256 devices in a mesh: item: 64 (over z_lo, y, x, core), week: 4 (over z_hi).
Axes of the slice: x: 4, y: 4, z: 8 (z_hi: 4, z_lo: 2; z = z_hi * 2 + z_lo), core: 2. Of those that a mesh axis runs over, the one named last changes fastest.
Arguments:
- counts: int32 [128, 256, 16384], P(None, 'week', 'item'), may hold values from 0 to 7, as said below
- user_factor: float32 [128, 64], replicated, may hold values from 0.3 to 1.5
- item_factor: float32 [16384, 64], P('item'), may hold values from 0.001 to 12, as said below
- week_factor: float32 [256, 64], P('week'), may hold values from 0.001 to 1.5, as said below
Outputs:
- updated_users: float32 [128, 64], replicated
The draws below stay inside these ranges and needn't reach their ends.
Inputs may be any that keep to these rules, and one draw needn't show every extreme that they name: `counts`: every user has at least one positive count. `item_factor`: positive entries. `week_factor`: positive entries.
All inputs are finite; a program needn't handle non-finite values.
Results may differ from the reference program's by a relative error of at most 0.0003.
Values sent between devices are 32-bit elements; how exact they have to be, the bound alone decides.
A program may use at most 128 MiB of HBM per device.

```python
import math
import jax
import jax.numpy as jnp
from jax import lax

USERS = 128
ITEMS = 16384
WEEKS = 256
RANK = 64
ITERS = 3


def item_groups(key):
    group_key = jax.random.fold_in(key, 5)
    return jax.random.randint(group_key, (ITEMS,), 0, RANK)


def positive_field(key, length, field_scale):
    base = jnp.exp(jax.random.uniform(key, (length, RANK), jnp.float32, math.log(0.3), math.log(3.0)))
    rise = 2.0
    position = jnp.arange(length, dtype=jnp.float32)[:, None] / max(length - 1, 1)
    return field_scale * base * (1.0 + rise * position)


def draw_item_factor(key, part):
    groups = item_groups(key)
    key = jax.random.fold_in(key, 11)
    base = positive_field(key, ITEMS, 0.04)
    column_index = jnp.arange(RANK, dtype=jnp.int32)[None, :]
    favoured = (groups[:, None] == column_index).astype(jnp.float32)
    return base * (1.0 + 20.0 * favoured)


def draw_week_factor(key, part):
    key = jax.random.fold_in(key, 23)
    return positive_field(key, WEEKS, 0.05)


def draw_counts(key, part):
    groups = item_groups(key)
    key = jax.random.fold_in(key, 37)
    taste_key, weekly_key, anchor_key, moment_key = jax.random.split(key, 4)
    liked = jax.random.randint(taste_key, (USERS, RANK), 0, 2)
    liked_items = liked[:, groups]
    anchor = jax.random.randint(anchor_key, (USERS, 1, 1), 0, ITEMS)
    week_anchor = jax.random.randint(moment_key, (USERS, 1, 1), 0, WEEKS)
    item_index = jnp.arange(ITEMS, dtype=jnp.int32)[None, None, :]
    week_index = jnp.arange(WEEKS, dtype=jnp.int32)[None, :, None]
    strong = jnp.maximum(jax.random.randint(weekly_key, (USERS, WEEKS, ITEMS), 0, 17) - 9, 0)
    faint = jnp.where(strong == 7, 1, 0)
    result = jnp.where(liked_items[:, None, :] == 1, strong, faint)
    result = jnp.where((item_index == anchor) & (week_index == week_anchor), 7, result)
    return result.astype(jnp.int32)


def setup_inputs(seed: int = 0) -> dict:
    streams_of = jax.random.split(jax.random.key(seed), 5)
    counts = draw_counts(jax.random.fold_in(streams_of[4], 71), 0)
    user_factor = jnp.clip(jnp.exp(jax.random.uniform(streams_of[1], (USERS, RANK), jnp.float32, math.log(0.3), math.log(1.5))), 0.3, 1.5)
    item_factor = draw_item_factor(jax.random.fold_in(streams_of[4], 71), 0)
    week_factor = draw_week_factor(jax.random.fold_in(streams_of[4], 71), 0)
    return {"counts": counts, "user_factor": user_factor, "item_factor": item_factor, "week_factor": week_factor}


def block_phi(factor, counts, item_factor, week_factor):
    item_block = min(256, ITEMS)
    blocks = ITEMS // item_block

    def accumulate(total, index):
        start = (index * item_block).astype(jnp.int32)
        block_counts = lax.dynamic_slice_in_dim(counts, start, item_block, 2)
        block_items = lax.dynamic_slice_in_dim(item_factor, start, item_block, 0)
        khatri_rao = (week_factor[:, None, :] * block_items[None, :, :]).reshape(-1, RANK)
        model = jnp.dot(factor, khatri_rao.T, precision=lax.Precision.HIGHEST)
        ratio = block_counts.reshape(USERS, -1).astype(jnp.float32) / model
        return total + jnp.dot(ratio, khatri_rao, precision=lax.Precision.HIGHEST), None

    start_total = jnp.zeros((USERS, RANK), jnp.float32)
    total, unused = lax.scan(accumulate, start_total, jnp.arange(blocks, dtype=jnp.int32))
    return total


def reference(counts, user_factor, item_factor, week_factor):
    denominator = jnp.sum(item_factor, axis=0) * jnp.sum(week_factor, axis=0)
    factor = user_factor
    for iteration in range(ITERS):
        phi = block_phi(factor, counts, item_factor, week_factor)
        factor = factor * phi / denominator[None, :]
    return factor
```

```python
import functools

import jax
import jax.numpy as jnp
from jax import lax
from jax.experimental import pallas as pl
from jax.experimental.pallas import tpu as pltpu
from jax.sharding import PartitionSpec as P

MESH = pl.DeviceIdType.MESH
F32, BF16 = jnp.float32, jnp.bfloat16
ITERS = 3
USERS, RANK, WEEKS, ITEMS = 128, 64, 64, 256
HALF, CHUNK, BLOCK = 64, 32, 16
CHUNKS = HALF // CHUNK
PACK = CHUNK // 2
X, Y, Z = 4, 4, 8


def by_distance(offsets, sizes):
    far = lambda o: sum(min(d, n - d) for d, n in zip(o, sizes))
    return sorted(offsets, key=far, reverse=True)


PLANE = by_distance([(dx, dy) for dx in range(X) for dy in range(Y) if dx or dy], (X, Y))
RING = by_distance([(dz,) for dz in range(1, Z)], (Z,))


def rows_of(step, chunk):
    return PACK + 8 if step == 0 and chunk == 0 else PACK


def kernel(
    counts_hbm, user_hbm, item_hbm, week_hbm, out_ref,
    counts, user, items, week, pair_week, model_rhs, phi_rhs, models, factor, phi,
    half_src, half_dst, plane, ring, last_src, last_dst,
    load_sem, count_sem, item_sems, swap_send, swap_recv,
    half_send, half_recv, plane_send, plane_recv, ring_send, ring_recv, last_send, last_recv,
):
    item, z_hi = lax.axis_index("item"), lax.axis_index("week")
    core, flat = lax.rem(item, 2), lax.rem(item // 2, X * Y)
    x, y = lax.rem(flat, X), flat // X
    z = z_hi * 2 + item // (2 * X * Y)
    other = {"item": item + 1 - 2 * core, "week": z_hi}

    def in_plane(dx, dy):
        there = lax.rem(y + dy, Y) * X + lax.rem(x + dx, X)
        return {"item": item + (there - flat) * 2, "week": z_hi}

    def in_ring(dz):
        there = lax.rem(z + dz, Z)
        return {"item": lax.rem(there, 2) * (2 * X * Y) + flat * 2 + core, "week": there // 2}

    plane_peers = [in_plane(*o) for o in PLANE]
    ring_peers = [in_ring(*o) for o in RING]
    barrier = pltpu.get_barrier_semaphore()
    for peer in [other, *plane_peers, *ring_peers]:
        pl.semaphore_signal(barrier, inc=1, device_id=peer, device_id_type=MESH)

    def remote(src, dst, send, recv, peer):
        return pltpu.make_async_remote_copy(
            src_ref=src, dst_ref=dst, send_sem=send, recv_sem=recv, device_id=peer, device_id_type=MESH
        )

    own_first, other_first = core * HALF, (1 - core) * HALF

    loads = [
        pltpu.make_async_copy(src, dst, load_sem.at[i])
        for i, (src, dst) in enumerate(((item_hbm, items.at[0]), (week_hbm, week), (user_hbm, user)))
    ]
    for load in loads:
        load.start()
    first_blocks = []
    for chunk in range(CHUNKS):
        starts = [first + chunk * CHUNK + b * BLOCK for first in (other_first, own_first) for b in range(CHUNK // BLOCK)]
        first_blocks.append([pl.multiple_of(s, BLOCK) for s in starts])
    count_loads = []
    for chunk in range(CHUNKS):
        for b, start in enumerate(first_blocks[chunk]):
            at = pl.ds(start, BLOCK)
            load = pltpu.make_async_copy(counts_hbm.at[at], counts.at[at], count_sem.at[chunk * 4 + b])
            load.start()
            count_loads.append(load)
    for load in loads:
        load.wait()

    lane = lax.broadcasted_iota(jnp.int32, (1, 2 * RANK), 1)
    left = lane < RANK
    low_lanes = jnp.where(left, 0.0, 1.0).astype(F32)

    def build_rhs(which):
        values = items[which]
        high = values.astype(BF16).astype(F32)
        both = jnp.concatenate([high, values - high], axis=1)
        phi_rhs[which] = both.astype(BF16)
        turned = both.T
        high, low = turned[:RANK], turned[RANK:]
        model_rhs[which] = jnp.concatenate([high, high, low, low], axis=0).astype(BF16)

    build_rhs(0)
    weeks = week[...]
    pair_week[...] = jnp.concatenate([weeks, weeks], axis=1)
    share = jnp.sum(items[0], axis=0, keepdims=True) * jnp.sum(weeks, axis=0, keepdims=True)
    share = jnp.broadcast_to(jnp.concatenate([share, share], axis=1), (8, 2 * RANK))

    packed = {}
    for chunk in range(CHUNKS):
        for half, first in enumerate((own_first, other_first)):
            rows = user[pl.ds(pl.multiple_of(first + chunk * CHUNK, CHUNK), CHUNK), :]
            factor[half, chunk] = jnp.concatenate([rows, rows], axis=1)
            if half == 0:
                packed[chunk] = jnp.concatenate([rows[:PACK], rows[PACK:]], axis=1)

    def model(block):
        _, half, chunk, row, which, _ = block
        w = pair_week[...]
        parts = []
        for u in range(BLOCK):
            scaled = factor[half, chunk, row + u : row + u + 1, :] * w
            high = scaled.astype(BF16).astype(F32)
            parts.append((scaled - high * low_lanes).astype(BF16))
        lhs = jnp.concatenate(parts, axis=0)
        return jnp.dot(jnp.concatenate([lhs, lhs], axis=1), model_rhs[which], preferred_element_type=F32)

    def accumulate(block, slot):
        start, half, _, row, which, add = block
        c = counts[pl.ds(start, BLOCK)].reshape(BLOCK * WEEKS, ITEMS).astype(F32)
        ratio = c * pl.reciprocal(models[slot], approx=False)
        high = ratio.astype(BF16)
        low = (ratio - high.astype(F32)).astype(BF16)
        rhs = phi_rhs[which]
        sums = jnp.dot(high, rhs, preferred_element_type=F32) + jnp.dot(low, rhs, preferred_element_type=F32)
        sums = jnp.sum(sums.reshape(BLOCK, WEEKS, 2 * RANK) * pair_week[...][None], axis=1)
        if add:
            sums = sums + phi[half, row : row + BLOCK, :]
        phi[half, row : row + BLOCK, :] = sums

    def pack(half):
        both = phi[half]
        both = both + pltpu.roll(both, RANK, 1)
        return jnp.where(left, both[:PACK], both[PACK:])

    def compute(blocks, before, after):
        before(0)
        models[0] = model(blocks[0])
        for j, block in enumerate(blocks):
            if j + 1 < len(blocks):
                coming = model(blocks[j + 1])
                before(j + 1)
            accumulate(block, j % 2)
            if j + 1 < len(blocks):
                models[(j + 1) % 2] = coming
            after(j)

    def send_half(chunk):
        n = rows_of(0, chunk)
        half_src[chunk, :PACK] = pack(1)
        if n > PACK:
            half_src[chunk, PACK:n] = share
        at = pl.ds(0, n)
        remote(half_src.at[chunk, at], half_dst.at[chunk, at], half_send.at[chunk], half_recv.at[chunk], other).start()

    def wait_bytes(ref, sem):
        pltpu.make_async_copy(ref, ref, sem).wait()

    def send_plane(step, chunk):
        n = rows_of(step, chunk)
        mine = pack(0)
        if step == 0:
            wait_bytes(half_dst.at[chunk, pl.ds(0, n)], half_recv.at[chunk])
            mine = mine + half_dst[chunk, :PACK]
            if n > PACK:
                plane[step, chunk, flat, PACK:n] = share + half_dst[chunk, PACK:n]
        plane[step, chunk, flat, :PACK] = mine
        block = plane.at[step, chunk, flat, pl.ds(0, n)]
        for peer in plane_peers:
            remote(block, block, plane_send.at[step, chunk], plane_recv.at[step, chunk], peer).start()

    def total(ref, step, chunk, n, count):
        parts = [ref[step, chunk, j, :n] for j in range(count)]
        while len(parts) > 1:
            parts = [a + b for a, b in zip(parts[::2], parts[1::2])]
        return parts[0]

    def send_ring(step, chunk):
        n = rows_of(step, chunk)
        wait_bytes(plane.at[step, chunk, pl.ds(0, X * Y - 1), pl.ds(0, n)], plane_recv.at[step, chunk])
        ring[step, chunk, z, :n] = total(plane, step, chunk, n, X * Y)
        block = ring.at[step, chunk, z, pl.ds(0, n)]
        for peer in ring_peers:
            remote(block, block, ring_send.at[step, chunk], ring_recv.at[step, chunk], peer).start()

    denominator = {}

    def update(step, chunk):
        n = rows_of(step, chunk)
        wait_bytes(ring.at[step, chunk, pl.ds(0, Z - 1), pl.ds(0, n)], ring_recv.at[step, chunk])
        sums = total(ring, step, chunk, n, Z)
        if n > PACK:
            denominator[0] = sums[PACK : PACK + 1]
        packed[chunk] = packed[chunk] * sums[:PACK] / denominator[0]
        if step < ITERS - 1:
            turned = pltpu.roll(packed[chunk], RANK, 1)
            factor[0, chunk, :PACK] = jnp.where(left, packed[chunk], turned)
            factor[0, chunk, PACK:] = jnp.where(left, turned, packed[chunk])

    def first(chunk):
        blocks = [
            (start, 1 - b // 2, chunk, (b % 2) * BLOCK, 0, False) for b, start in enumerate(first_blocks[chunk])
        ]

        def after(j):
            if j == 1:
                if chunk == 0:
                    pl.semaphore_wait(barrier, 1 + len(plane_peers) + len(ring_peers))
                    remote(items.at[0], items.at[1], item_sems.at[0], item_sems.at[1], other).start()
                send_half(chunk)

        compute(blocks, lambda j: count_loads[chunk * 4 + j].wait(), after)

    first(0)
    send_plane(0, 0)
    first(1)
    swaps = []
    for chunk in range(CHUNKS):
        theirs = pl.ds(pl.multiple_of(other_first + chunk * CHUNK, CHUNK), CHUNK)
        landing = pl.ds(USERS + chunk * CHUNK, CHUNK)
        swap = remote(counts_hbm.at[theirs], counts.at[landing], swap_send.at[chunk], swap_recv.at[chunk], other)
        swap.start()
        swaps.append(swap)
    send_plane(0, 1)
    wait_bytes(items.at[1], item_sems.at[1])
    build_rhs(1)
    send_ring(0, 0)
    send_ring(0, 1)
    update(0, 0)

    def later(chunk):
        own = pl.multiple_of(own_first + chunk * CHUNK, CHUNK)
        starts = [own, own + BLOCK, USERS + chunk * CHUNK, USERS + chunk * CHUNK + BLOCK]
        blocks = [(start, 0, chunk, (b % 2) * BLOCK, b // 2, b >= 2) for b, start in enumerate(starts)]
        compute(blocks, lambda j: None, lambda j: None)

    for step in range(1, ITERS):
        if step == 1:
            swaps[0].wait_recv()
        later(0)
        send_plane(step, 0)
        update(step - 1, 1)
        if step == 1:
            swaps[1].wait_recv()
        later(1)
        send_plane(step, 1)
        send_ring(step, 0)
        send_ring(step, 1)
        update(step, 0)
        if step == ITERS - 1:
            send_last = []
            for chunk in range(CHUNKS):
                if chunk:
                    update(step, chunk)
                last_src[chunk] = packed[chunk]
                copy = remote(last_src.at[chunk], last_dst.at[chunk], last_send.at[chunk], last_recv.at[chunk], other)
                copy.start()
                send_last.append(copy)

    def write(first, chunk, rows):
        at = first + chunk * CHUNK
        out_ref[pl.ds(pl.multiple_of(at, PACK), PACK), :] = rows[:, :RANK]
        out_ref[pl.ds(pl.multiple_of(at + PACK, PACK), PACK), :] = rows[:, RANK:]

    for chunk in range(CHUNKS):
        write(own_first, chunk, packed[chunk])
    for chunk in range(CHUNKS):
        send_last[chunk].wait_recv()
        write(other_first, chunk, last_dst[chunk])

    wait_bytes(items.at[0], item_sems.at[0])
    for chunk in range(CHUNKS):
        send_last[chunk].wait_send()
        swaps[chunk].wait_send()
        wait_bytes(half_src.at[chunk, pl.ds(0, rows_of(0, chunk))], half_send.at[chunk])
        for step in range(ITERS):
            n = pl.ds(0, rows_of(step, chunk))
            wait_bytes(plane.at[step, chunk, pl.ds(0, X * Y - 1), n], plane_send.at[step, chunk])
            wait_bytes(ring.at[step, chunk, pl.ds(0, Z - 1), n], ring_send.at[step, chunk])


def per_device(counts, user_factor, item_factor, week_factor):
    most = PACK + 8
    dma = pltpu.SemaphoreType.DMA
    return pl.pallas_call(
        kernel,
        out_shape=jax.ShapeDtypeStruct((USERS, RANK), F32),
        in_specs=[pl.BlockSpec(memory_space=pl.ANY)] * 4,
        out_specs=pl.BlockSpec(memory_space=pltpu.VMEM),
        scratch_shapes=[
            pltpu.VMEM((USERS + HALF, WEEKS, ITEMS), jnp.int32),
            pltpu.VMEM((USERS, RANK), F32),
            pltpu.VMEM((2, ITEMS, RANK), F32),
            pltpu.VMEM((WEEKS, RANK), F32),
            pltpu.VMEM((WEEKS, 2 * RANK), F32),
            pltpu.VMEM((2, 4 * RANK, ITEMS), BF16),
            pltpu.VMEM((2, ITEMS, 2 * RANK), BF16),
            pltpu.VMEM((2, BLOCK * WEEKS, ITEMS), F32),
            pltpu.VMEM((2, CHUNKS, CHUNK, 2 * RANK), F32),
            pltpu.VMEM((2, CHUNK, 2 * RANK), F32),
            pltpu.VMEM((CHUNKS, most, 2 * RANK), F32),
            pltpu.VMEM((CHUNKS, most, 2 * RANK), F32),
            pltpu.VMEM((ITERS, CHUNKS, X * Y, most, 2 * RANK), F32),
            pltpu.VMEM((ITERS, CHUNKS, Z, most, 2 * RANK), F32),
            pltpu.VMEM((CHUNKS, PACK, 2 * RANK), F32),
            pltpu.VMEM((CHUNKS, PACK, 2 * RANK), F32),
            dma((3,)), dma((CHUNKS * 4,)), dma((2,)), dma((CHUNKS,)), dma((CHUNKS,)),
            dma((CHUNKS,)), dma((CHUNKS,)), dma((ITERS, CHUNKS)), dma((ITERS, CHUNKS)),
            dma((ITERS, CHUNKS)), dma((ITERS, CHUNKS)), dma((CHUNKS,)), dma((CHUNKS,)),
        ],
        compiler_params=pltpu.CompilerParams(
            collective_id=0, has_side_effects=True, vmem_limit_bytes=40 << 20
        ),
        name="updates",
    )(counts, user_factor, item_factor, week_factor)


def solution(mesh):
    placed = (P(None, "week", "item"), P(), P("item", None), P("week", None))
    return jax.shard_map(per_device, mesh=mesh, in_specs=placed, out_specs=P(), check_vma=False)
```

```python
import jax
import jax.numpy as jnp
from jax import lax
from jax.experimental import pallas as pl
from jax.experimental.pallas import tpu as pltpu
from jax.sharding import PartitionSpec as P

MESH = pl.DeviceIdType.MESH
F32, BF16 = jnp.float32, jnp.bfloat16
ITERS = 3
USERS, RANK, WEEKS, ITEMS = 128, 64, 64, 256
HALF, CHUNK, BLOCK = 64, 32, 16
CHUNKS, BLOCKS = HALF // CHUNK, CHUNK // BLOCK
PACK = CHUNK // 2
X, Y, Z = 4, 4, 8
FULL = X * Y


def by_distance(offsets, sizes):
    far = lambda o: sum(min(d, n - d) for d, n in zip(o, sizes))
    return sorted(offsets, key=far, reverse=True)


PLANE = by_distance([(dx, dy) for dx in range(X) for dy in range(Y)], (X, Y))
RING = by_distance([(dz,) for dz in range(Z)], (Z,))


def rows_of(step, chunk):
    return PACK + 8 if step == 0 and chunk == 0 else PACK


def kernel(
    counts_hbm, user_hbm, item_hbm, week_hbm, out_ref,
    counts, user_turned, user, items, week, pair_week, model_rhs, phi_rhs, models, factor, phi, held,
    half_src, half_dst, plane, ring,
    load_sem, count_sem, item_sems, swap_send, swap_recv, held_send, held_recv,
    half_send, half_recv, plane_send, plane_recv, ring_send, ring_recv,
):
    item, z_hi = lax.axis_index("item"), lax.axis_index("week")
    core, flat = lax.rem(item, 2), lax.rem(item // 2, FULL)
    x, y = lax.rem(flat, X), flat // X
    z = z_hi * 2 + item // (2 * FULL)

    def on(c):
        return pl.when(core == c)

    def in_plane(c, dx, dy):
        there = lax.rem(y + dy, Y) * X + lax.rem(x + dx, X)
        return {"item": item - core + c + (there - flat) * 2, "week": z_hi}

    def in_ring(c, dz):
        there = lax.rem(z + dz, Z)
        return {"item": lax.rem(there, 2) * (2 * FULL) + flat * 2 + c, "week": there // 2}

    other = in_ring(1 - core, 0)
    plane_peers = [[in_plane(c, *o) for o in PLANE] for c in range(2)]
    ring_peers = [[in_ring(c, *o) for o in RING] for c in range(2)]

    barrier = pltpu.get_barrier_semaphore()

    def greet(peers):
        for peer in peers:
            pl.semaphore_signal(barrier, inc=1, device_id=peer, device_id_type=MESH)

    @on(0)
    def _():
        greet(ring_peers[1])

    @on(1)
    def _():
        greet(plane_peers[0][:-1] + plane_peers[1][:-1] + ring_peers[1][:-1] + plane_peers[0][-1:])

    def remote(src, dst, send, recv, peer):
        return pltpu.make_async_remote_copy(
            src_ref=src, dst_ref=dst, send_sem=send, recv_sem=recv, device_id=peer, device_id_type=MESH
        )

    loads = [
        pltpu.make_async_copy(src, dst, load_sem.at[i])
        for i, (src, dst) in enumerate(((item_hbm, items.at[0]), (week_hbm, week), (user_hbm, user_turned)))
    ]
    for load in loads:
        load.start()
    first_blocks = [
        (chunk, half, b * BLOCK) for chunk in range(CHUNKS) for half in range(2) for b in range(BLOCKS)
    ]
    count_loads = []
    for i, (chunk, half, row) in enumerate(first_blocks):
        at = pl.ds(half * HALF + chunk * CHUNK + row, BLOCK)
        load = pltpu.make_async_copy(counts_hbm.at[at], counts.at[at], count_sem.at[i])
        load.start()
        count_loads.append(load)
    for load in loads:
        load.wait()

    left = lax.broadcasted_iota(jnp.int32, (1, 2 * RANK), 1) < RANK
    low_lanes = jnp.where(left, 0.0, 1.0).astype(F32)

    def build_rhs(which):
        values = items[which]
        high = values.astype(BF16).astype(F32)
        low = values - high
        model_rhs[which] = jnp.concatenate([high, high, low, low], axis=0).astype(BF16)
        both = jnp.concatenate([high, low], axis=0).T
        phi_rhs[which] = both.astype(BF16)
        sums = jnp.sum(both, axis=0, keepdims=True)
        return sums + pltpu.roll(sums, RANK, 1)

    item_sums = build_rhs(0)
    weeks = week[...]
    pair_week[...] = jnp.concatenate([weeks, weeks], axis=1)
    share = jnp.broadcast_to(item_sums * jnp.sum(pair_week[...], axis=0, keepdims=True), (8, 2 * RANK))
    user[...] = user_turned[...].T

    for half in range(2):
        for chunk in range(CHUNKS):
            rows = user[half * HALF + chunk * CHUNK : half * HALF + (chunk + 1) * CHUNK, :]
            factor[half, chunk] = jnp.concatenate([rows, rows], axis=1)
            held[half, chunk] = jnp.concatenate([rows[:PACK], rows[PACK:]], axis=1)

    def model(block):
        _, half, chunk, row, which, _, _ = block
        w = pair_week[...]
        parts = []
        for u in range(BLOCK):
            scaled = factor[half, chunk, row + u : row + u + 1, :] * w
            high = scaled.astype(BF16).astype(F32)
            parts.append((scaled - high * low_lanes).astype(BF16))
        lhs = jnp.concatenate(parts, axis=0)
        return jnp.dot(jnp.concatenate([lhs, lhs], axis=1), model_rhs[which], preferred_element_type=F32)

    def accumulate(block, slot):
        start, _, _, row, which, into, add = block
        c = counts[pl.ds(start, BLOCK)].reshape(BLOCK * WEEKS, ITEMS).astype(F32)
        ratio = c * pl.reciprocal(models[slot], approx=False)
        high = ratio.astype(BF16)
        low = (ratio - high.astype(F32)).astype(BF16)
        rhs = phi_rhs[which]
        sums = jnp.dot(high, rhs, preferred_element_type=F32) + jnp.dot(low, rhs, preferred_element_type=F32)
        sums = jnp.sum(sums.reshape(BLOCK, WEEKS, 2 * RANK) * pair_week[...][None], axis=1)
        if add:
            sums = sums + phi[into, row : row + BLOCK, :]
        phi[into, row : row + BLOCK, :] = sums

    def pack(half):
        both = phi[half]
        both = both + pltpu.roll(both, RANK, 1)
        return jnp.where(left, both[:PACK], both[PACK:])

    def compute(blocks, before, after):
        before(0)
        models[0] = model(blocks[0])
        for j, block in enumerate(blocks):
            if j + 1 < len(blocks):
                coming = model(blocks[j + 1])
                before(j + 1)
            accumulate(block, j % 2)
            if j + 1 < len(blocks):
                models[(j + 1) % 2] = coming
            after(j)

    def wait_bytes(ref, sem):
        pltpu.make_async_copy(ref, ref, sem).wait()

    def total(parts):
        while len(parts) > 1:
            parts = [a + b for a, b in zip(parts[::2], parts[1::2])]
        return parts[0]

    def share_half(chunk, half):
        n = rows_of(0, chunk)
        mine = pack(half)
        half_src[chunk, half, :PACK] = mine
        if n > PACK:
            half_src[chunk, half, PACK:n] = share

        @on(0)
        def _():
            at = pl.ds(0, n)
            remote(
                half_src.at[chunk, half, at], half_dst.at[chunk, half, at],
                half_send.at[chunk, half], half_recv.at[chunk, half], other,
            ).start()

    def send_first(chunk, half):
        n = rows_of(0, chunk)

        @on(1)
        def _():
            wait_bytes(half_dst.at[chunk, half, pl.ds(0, n)], half_recv.at[chunk, half])
            plane[0, chunk, half, flat, :n] = half_src[chunk, half, :n] + half_dst[chunk, half, :n]
            block = plane.at[0, chunk, half, flat, pl.ds(0, n)]
            for peer in plane_peers[1][:-1]:
                remote(block, block, plane_send.at[0, chunk, half], plane_recv.at[0, chunk, half], peer).start()

    def send_plane(step, chunk):
        plane[step, chunk, core, flat, :PACK] = pack(0)
        for c, peers in ((0, plane_peers[1]), (1, plane_peers[1][:-1])):

            @on(c)
            def _():
                block = plane.at[step, chunk, c, flat, pl.ds(0, PACK)]
                for peer in peers:
                    remote(block, block, plane_send.at[step, chunk, c], plane_recv.at[step, chunk, c], peer).start()

    def ring_targets(step, half):
        last = step == ITERS - 1
        return (ring_peers[0] if last or half == 0 else []) + (ring_peers[1][:-1] if last or half == 1 else [])

    def send_ring(step, chunk, half):
        n = rows_of(step, chunk)

        @on(1)
        def _():
            arriving = FULL if step and half == 0 else FULL - 1
            wait_bytes(plane.at[step, chunk, half, pl.ds(0, arriving), pl.ds(0, n)], plane_recv.at[step, chunk, half])
            ring[step, chunk, half, z, :n] = total([plane[step, chunk, half, j, :n] for j in range(FULL)])
            block = ring.at[step, chunk, half, z, pl.ds(0, n)]
            for peer in ring_targets(step, half):
                remote(block, block, ring_send.at[step, chunk, half], ring_recv.at[step, chunk, half], peer).start()

    def wait_ring(step, chunk, c, half):
        at = pl.ds(0, Z - c), pl.ds(0, rows_of(step, chunk))
        wait_bytes(ring.at[(step, chunk, half, *at)], ring_recv.at[step, chunk, half])

    denominator = {}

    def update(step, chunk):
        n = rows_of(step, chunk)
        for c in range(2):

            @on(c)
            def _():
                wait_ring(step, chunk, c, c)

        sums = total([ring[step, chunk, core, j, :n] for j in range(Z)])
        if n > PACK:
            denominator[0] = sums[PACK : PACK + 1]
        new = held[core, chunk] * sums[:PACK] / denominator[0]
        held[core, chunk] = new
        turned = pltpu.roll(new, RANK, 1)
        factor[core, chunk, :PACK] = jnp.where(left, new, turned)
        factor[core, chunk, PACK:] = jnp.where(left, turned, new)
        if step == ITERS - 2:
            mine = held.at[core, chunk]
            remote(mine, mine, held_send.at[chunk], held_recv.at[chunk], other).start()

    def before_first(j):
        count_loads[j].wait()

    def after_first(j):
        chunk, half, row = first_blocks[j]
        if row + BLOCK < CHUNK:
            return
        if chunk == 0 and half == 0:
            for c, n in ((0, FULL), (1, FULL - 1 + Z - 1 + Z)):

                @on(c)
                def _():
                    pl.semaphore_wait(barrier, n)

            remote(items.at[0], items.at[1], item_sems.at[0], item_sems.at[1], other).start()
        share_half(chunk, half)
        if half:
            send_first(chunk, 0)
        elif chunk:
            send_first(chunk - 1, 1)

    blocks = [
        (half * HALF + chunk * CHUNK + row, half, chunk, row, 0, half, False) for chunk, half, row in first_blocks
    ]
    compute(blocks, before_first, after_first)
    swaps = []
    for chunk in range(CHUNKS):
        theirs = pl.ds(pl.multiple_of((1 - core) * HALF + chunk * CHUNK, CHUNK), CHUNK)
        landing = pl.ds(USERS + chunk * CHUNK, CHUNK)
        swap = remote(counts_hbm.at[theirs], counts.at[landing], swap_send.at[chunk], swap_recv.at[chunk], other)
        swap.start()
        swaps.append(swap)
    wait_bytes(items.at[1], item_sems.at[1])
    build_rhs(1)
    send_first(CHUNKS - 1, 1)
    for chunk in range(CHUNKS):
        for half in range(2):
            send_ring(0, chunk, half)

    def later(chunk):
        own = pl.multiple_of(core * HALF + chunk * CHUNK, CHUNK)
        blocks = [
            (start + row, core, chunk, row, which, 0, which > 0)
            for which, start in enumerate((own, USERS + chunk * CHUNK))
            for row in range(0, CHUNK, BLOCK)
        ]
        compute(blocks, lambda j: None, lambda j: None)

    for step in range(1, ITERS):
        for chunk in range(CHUNKS):
            update(step - 1, chunk)
            if step == 1:
                swaps[chunk].wait_recv()
            later(chunk)
            send_plane(step, chunk)
        for chunk in range(CHUNKS):
            send_ring(step, chunk, 1)
            send_ring(step, chunk, 0)

    for chunk in range(CHUNKS):
        wait_bytes(held.at[0, chunk], held_recv.at[chunk])
        for half in (1, 0):
            for c in range(2):

                @on(c)
                def _():
                    wait_ring(ITERS - 1, chunk, c, half)

            sums = total([ring[ITERS - 1, chunk, half, j, :PACK] for j in range(Z)])
            new = held[half, chunk] * sums / denominator[0]
            at = half * HALF + chunk * CHUNK
            user[at : at + PACK, :] = new[:, :RANK]
            user[at + PACK : at + CHUNK, :] = new[:, RANK:]
    out_ref[...] = user[...].T

    wait_bytes(items.at[0], item_sems.at[0])
    for chunk in range(CHUNKS):
        swaps[chunk].wait_send()
        wait_bytes(held.at[0, chunk], held_send.at[chunk])

    def wait_sent(step, chunk, half, blocks, sem):
        if blocks:
            at = pl.ds(0, blocks), pl.ds(0, rows_of(step, chunk))
            wait_bytes(plane.at[(step, chunk, half, *at)], sem.at[step, chunk, half])

    @on(0)
    def _():
        for chunk in range(CHUNKS):
            for half in range(2):
                wait_bytes(half_src.at[chunk, half, pl.ds(0, rows_of(0, chunk))], half_send.at[chunk, half])
            for step in range(1, ITERS):
                wait_sent(step, chunk, 0, FULL, plane_send)

    @on(1)
    def _():
        for chunk in range(CHUNKS):
            for step in range(ITERS):
                for half in range(2):
                    wait_sent(step, chunk, half, FULL - 1 if half or not step else 0, plane_send)
                    wait_sent(step, chunk, half, len(ring_targets(step, half)), ring_send)


def per_device(counts, user_factor, item_factor, week_factor):
    most = PACK + 8
    dma = pltpu.SemaphoreType.DMA
    each = (ITERS, CHUNKS, 2)
    arrays = counts, user_factor.T, item_factor.T, week_factor
    turned = pl.pallas_call(
        kernel,
        out_shape=pltpu.VMEM((RANK, USERS), F32),
        in_specs=[pl.BlockSpec(memory_space=pltpu.HBM)] * 4,
        out_specs=pl.BlockSpec(memory_space=pltpu.VMEM),
        scratch_shapes=[
            pltpu.VMEM((USERS + HALF, WEEKS, ITEMS), jnp.int32),
            pltpu.VMEM((RANK, USERS), F32),
            pltpu.VMEM((USERS, RANK), F32),
            pltpu.VMEM((2, RANK, ITEMS), F32),
            pltpu.VMEM((WEEKS, RANK), F32),
            pltpu.VMEM((WEEKS, 2 * RANK), F32),
            pltpu.VMEM((2, 4 * RANK, ITEMS), BF16),
            pltpu.VMEM((2, ITEMS, 2 * RANK), BF16),
            pltpu.VMEM((2, BLOCK * WEEKS, ITEMS), F32),
            pltpu.VMEM((2, CHUNKS, CHUNK, 2 * RANK), F32),
            pltpu.VMEM((2, CHUNK, 2 * RANK), F32),
            pltpu.VMEM((2, CHUNKS, PACK, 2 * RANK), F32),
            pltpu.VMEM((CHUNKS, 2, most, 2 * RANK), F32),
            pltpu.VMEM((CHUNKS, 2, most, 2 * RANK), F32),
            pltpu.VMEM((*each, FULL, most, 2 * RANK), F32),
            pltpu.VMEM((*each, Z, most, 2 * RANK), F32),
            dma((3,)), dma((len(range(0, USERS, BLOCK)),)), dma((2,)), dma((CHUNKS,)), dma((CHUNKS,)),
            dma((CHUNKS,)), dma((CHUNKS,)), dma((CHUNKS, 2)), dma((CHUNKS, 2)),
            dma(each), dma(each), dma(each), dma(each),
        ],
        compiler_params=pltpu.CompilerParams(
            collective_id=0, has_side_effects=True, vmem_limit_bytes=48 << 20
        ),
        name="updates",
    )(*[pltpu.with_memory_space_constraint(a, pltpu.HBM) for a in arrays])
    return turned.T


def solution(mesh):
    placed = (P(None, "week", "item"), P(), P("item", None), P("week", None))
    return jax.shard_map(per_device, mesh=mesh, in_specs=placed, out_specs=P(), check_vma=False)
```

```python
import jax
import jax.numpy as jnp
from jax import lax
from jax.experimental import pallas as pl
from jax.experimental.pallas import tpu as pltpu
from jax.sharding import PartitionSpec as P

MESH = pl.DeviceIdType.MESH
F32, BF16 = jnp.float32, jnp.bfloat16
ITERS = 3
USERS, RANK, WEEKS, ITEMS = 128, 64, 64, 256
HALF, CHUNK, BLOCK = 64, 32, 16
CHUNKS, BLOCKS = HALF // CHUNK, CHUNK // BLOCK
PACK = CHUNK // 2
X, Y, Z = 4, 4, 8
FULL = X * Y


def by_distance(offsets, sizes):
    far = lambda o: sum(min(d, n - d) for d, n in zip(o, sizes))
    return sorted(offsets, key=far, reverse=True)


PLANE = by_distance([(dx, dy) for dx in range(X) for dy in range(Y)], (X, Y))
RING = by_distance([(dz,) for dz in range(Z)], (Z,))


def rows_of(step, chunk):
    return PACK + 8 if step == 0 and chunk == 0 else PACK


def kernel(
    counts_hbm, user_hbm, item_hbm, week_hbm, out_ref,
    counts, user_turned, user, items, week, pair_week, model_rhs, phi_rhs, models, factor, phi, held, final,
    half_src, half_dst, plane, ring,
    load_sem, count_sem, item_sems, swap_send, swap_recv, held_send, held_recv, final_send, final_recv,
    half_send, half_recv, plane_send, plane_recv, ring_send, ring_recv,
):
    item, z_hi = lax.axis_index("item"), lax.axis_index("week")
    core, flat = lax.rem(item, 2), lax.rem(item // 2, FULL)
    x, y = lax.rem(flat, X), flat // X
    z = z_hi * 2 + item // (2 * FULL)

    def on(c):
        return pl.when(core == c)

    def in_plane(c, dx, dy):
        there = lax.rem(y + dy, Y) * X + lax.rem(x + dx, X)
        return {"item": item - core + c + (there - flat) * 2, "week": z_hi}

    def in_ring(c, dz):
        there = lax.rem(z + dz, Z)
        return {"item": lax.rem(there, 2) * (2 * FULL) + flat * 2 + c, "week": there // 2}

    other = in_ring(1 - core, 0)
    plane_peers = [[in_plane(c, *o) for o in PLANE] for c in range(2)]
    ring_peers = [[in_ring(c, *o) for o in RING] for c in range(2)]

    def remote(src, dst, send, recv, peer):
        return pltpu.make_async_remote_copy(
            src_ref=src, dst_ref=dst, send_sem=send, recv_sem=recv, device_id=peer, device_id_type=MESH
        )

    loads = [
        pltpu.make_async_copy(src, dst, load_sem.at[i])
        for i, (src, dst) in enumerate(((item_hbm, items.at[0]), (week_hbm, week), (user_hbm, user_turned)))
    ]
    for load in loads:
        load.start()
    barrier = pltpu.get_barrier_semaphore()

    def greet(peers):
        for peer in peers:
            pl.semaphore_signal(barrier, inc=1, device_id=peer, device_id_type=MESH)

    @on(0)
    def _():
        greet(ring_peers[1])

    @on(1)
    def _():
        greet(plane_peers[1][:-1] + ring_peers[1][:-1] + [other])

    first_blocks = [
        (chunk, half, b * BLOCK) for chunk in range(CHUNKS) for half in range(2) for b in range(BLOCKS)
    ]
    count_loads = []
    for i, (chunk, half, row) in enumerate(first_blocks):
        at = pl.ds(half * HALF + chunk * CHUNK + row, BLOCK)
        load = pltpu.make_async_copy(counts_hbm.at[at], counts.at[at], count_sem.at[i])
        load.start()
        count_loads.append(load)
    for load in loads:
        load.wait()

    left = lax.broadcasted_iota(jnp.int32, (1, 2 * RANK), 1) < RANK
    low_lanes = jnp.where(left, 0.0, 1.0).astype(F32)

    def build_rhs(which):
        values = items[which]
        high = values.astype(BF16).astype(F32)
        low = values - high
        model_rhs[which] = jnp.concatenate([high, high, low, low], axis=0).astype(BF16)
        both = jnp.concatenate([high, low], axis=0).T
        phi_rhs[which] = both.astype(BF16)
        sums = jnp.sum(both, axis=0, keepdims=True)
        return sums + pltpu.roll(sums, RANK, 1)

    item_sums = build_rhs(0)
    weeks = week[...]
    pair_week[...] = jnp.concatenate([weeks, weeks], axis=1)
    share = jnp.broadcast_to(item_sums * jnp.sum(pair_week[...], axis=0, keepdims=True), (8, 2 * RANK))
    user[...] = user_turned[...].T

    for half in range(2):
        for chunk in range(CHUNKS):
            rows = user[half * HALF + chunk * CHUNK : half * HALF + (chunk + 1) * CHUNK, :]
            factor[half, chunk] = jnp.concatenate([rows, rows], axis=1)
            held[half, chunk] = jnp.concatenate([rows[:PACK], rows[PACK:]], axis=1)

    def model(block):
        _, half, chunk, row, which, _, _ = block
        w = pair_week[...]
        parts = []
        for u in range(BLOCK):
            scaled = factor[half, chunk, row + u : row + u + 1, :] * w
            high = scaled.astype(BF16).astype(F32)
            parts.append((scaled - high * low_lanes).astype(BF16))
        lhs = jnp.concatenate(parts, axis=0)
        return jnp.dot(jnp.concatenate([lhs, lhs], axis=1), model_rhs[which], preferred_element_type=F32)

    def accumulate(block, slot):
        start, _, _, row, which, into, add = block
        c = counts[pl.ds(start, BLOCK)].reshape(BLOCK * WEEKS, ITEMS).astype(F32)
        ratio = c * pl.reciprocal(models[slot], approx=False)
        high = ratio.astype(BF16)
        low = (ratio - high.astype(F32)).astype(BF16)
        rhs = phi_rhs[which]
        sums = jnp.dot(high, rhs, preferred_element_type=F32) + jnp.dot(low, rhs, preferred_element_type=F32)
        sums = jnp.sum(sums.reshape(BLOCK, WEEKS, 2 * RANK) * pair_week[...][None], axis=1)
        if add:
            sums = sums + phi[into, row : row + BLOCK, :]
        phi[into, row : row + BLOCK, :] = sums

    def pack(half):
        both = phi[half]
        both = both + pltpu.roll(both, RANK, 1)
        return jnp.where(left, both[:PACK], both[PACK:])

    def compute(blocks, before, after):
        before(0)
        models[0] = model(blocks[0])
        for j, block in enumerate(blocks):
            if j + 1 < len(blocks):
                coming = model(blocks[j + 1])
                before(j + 1)
            accumulate(block, j % 2)
            if j + 1 < len(blocks):
                models[(j + 1) % 2] = coming
            after(j)

    def wait_bytes(ref, sem):
        pltpu.make_async_copy(ref, ref, sem).wait()

    def total(parts):
        while len(parts) > 1:
            parts = [a + b for a, b in zip(parts[::2], parts[1::2])]
        return parts[0]

    def share_half(chunk, half):
        n = rows_of(0, chunk)
        mine = pack(half)
        half_src[chunk, half, :PACK] = mine
        if n > PACK:
            half_src[chunk, half, PACK:n] = share

        @on(0)
        def _():
            at = pl.ds(0, n)
            remote(
                half_src.at[chunk, half, at], half_dst.at[chunk, half, at],
                half_send.at[chunk, half], half_recv.at[chunk, half], other,
            ).start()

    def send_first(chunk, half):
        n = rows_of(0, chunk)

        @on(1)
        def _():
            wait_bytes(half_dst.at[chunk, half, pl.ds(0, n)], half_recv.at[chunk, half])
            plane[0, chunk, half, flat, :n] = half_src[chunk, half, :n] + half_dst[chunk, half, :n]
            block = plane.at[0, chunk, half, flat, pl.ds(0, n)]
            for peer in plane_peers[1][:-1]:
                remote(block, block, plane_send.at[0, chunk, half], plane_recv.at[0, chunk, half], peer).start()

    def send_plane(step, chunk):
        plane[step, chunk, core, flat, :PACK] = pack(0)
        for c, peers in ((0, plane_peers[1]), (1, plane_peers[1][:-1])):

            @on(c)
            def _():
                block = plane.at[step, chunk, c, flat, pl.ds(0, PACK)]
                for peer in peers:
                    remote(block, block, plane_send.at[step, chunk, c], plane_recv.at[step, chunk, c], peer).start()

    def ring_targets(step, half):
        return ring_peers[0] if half == 0 and step < ITERS - 1 else ring_peers[1][:-1]

    def send_ring(step, chunk, half):
        n = rows_of(step, chunk)

        @on(1)
        def _():
            arriving = FULL if step and half == 0 else FULL - 1
            wait_bytes(plane.at[step, chunk, half, pl.ds(0, arriving), pl.ds(0, n)], plane_recv.at[step, chunk, half])
            ring[step, chunk, half, z, :n] = total([plane[step, chunk, half, j, :n] for j in range(FULL)])
            block = ring.at[step, chunk, half, z, pl.ds(0, n)]
            for peer in ring_targets(step, half):
                remote(block, block, ring_send.at[step, chunk, half], ring_recv.at[step, chunk, half], peer).start()

    def wait_ring(step, chunk, c, half):
        at = pl.ds(0, Z - c), pl.ds(0, rows_of(step, chunk))
        wait_bytes(ring.at[(step, chunk, half, *at)], ring_recv.at[step, chunk, half])

    denominator = {}

    def update(step, chunk):
        n = rows_of(step, chunk)
        for c in range(2):

            @on(c)
            def _():
                wait_ring(step, chunk, c, c)

        sums = total([ring[step, chunk, core, j, :n] for j in range(Z)])
        if n > PACK:
            denominator[0] = sums[PACK : PACK + 1]
        new = held[core, chunk] * sums[:PACK] / denominator[0]
        held[core, chunk] = new
        turned = pltpu.roll(new, RANK, 1)
        factor[core, chunk, :PACK] = jnp.where(left, new, turned)
        factor[core, chunk, PACK:] = jnp.where(left, turned, new)
        if step == ITERS - 2:

            @on(0)
            def _():
                mine = held.at[0, chunk]
                remote(mine, mine, held_send.at[chunk], held_recv.at[chunk], other).start()


    def before_first(j):
        count_loads[j].wait()

    def after_first(j):
        chunk, half, row = first_blocks[j]
        if row + BLOCK < CHUNK:
            return
        if chunk == 0 and half == 0:
            for c, n in ((0, 1), (1, FULL - 1 + Z - 1 + Z)):

                @on(c)
                def _():
                    pl.semaphore_wait(barrier, n)

        share_half(chunk, half)
        if half:
            send_first(chunk, 0)
        elif chunk:
            send_first(chunk - 1, 1)

    blocks = [
        (half * HALF + chunk * CHUNK + row, half, chunk, row, 0, half, False) for chunk, half, row in first_blocks
    ]
    compute(blocks, before_first, after_first)
    remote(items.at[0], items.at[1], item_sems.at[0], item_sems.at[1], other).start()
    swaps = []
    for chunk in range(CHUNKS):
        theirs = pl.ds(pl.multiple_of((1 - core) * HALF + chunk * CHUNK, CHUNK), CHUNK)
        landing = pl.ds(USERS + chunk * CHUNK, CHUNK)
        swap = remote(counts_hbm.at[theirs], counts.at[landing], swap_send.at[chunk], swap_recv.at[chunk], other)
        swap.start()
        swaps.append(swap)
    wait_bytes(items.at[1], item_sems.at[1])
    build_rhs(1)
    send_first(CHUNKS - 1, 1)
    for chunk in range(CHUNKS):
        for half in range(2):
            send_ring(0, chunk, half)

    def later(chunk):
        own = pl.multiple_of(core * HALF + chunk * CHUNK, CHUNK)
        blocks = [
            (start + row, core, chunk, row, which, 0, which > 0)
            for which, start in enumerate((own, USERS + chunk * CHUNK))
            for row in range(0, CHUNK, BLOCK)
        ]
        compute(blocks, lambda j: None, lambda j: None)

    for step in range(1, ITERS):
        for chunk in range(CHUNKS):
            update(step - 1, chunk)
            if step == 1:
                swaps[chunk].wait_recv()
            later(chunk)
            send_plane(step, chunk)
        for chunk in range(CHUNKS):
            send_ring(step, chunk, 1)
            send_ring(step, chunk, 0)

    @on(1)
    def _():
        for chunk in range(CHUNKS):
            wait_bytes(held.at[0, chunk], held_recv.at[chunk])
            for half in (1, 0):
                wait_ring(ITERS - 1, chunk, 1, half)
                sums = total([ring[ITERS - 1, chunk, half, j, :PACK] for j in range(Z)])
                final[half, chunk] = held[half, chunk] * sums / denominator[0]
                mine = final.at[half, chunk]
                remote(mine, mine, final_send.at[chunk, half], final_recv.at[chunk, half], other).start()

    @on(0)
    def _():
        for chunk in range(CHUNKS):
            for half in (1, 0):
                wait_bytes(final.at[half, chunk], final_recv.at[chunk, half])

    for chunk in range(CHUNKS):
        for half in range(2):
            new = final[half, chunk]
            at = half * HALF + chunk * CHUNK
            user[at : at + PACK, :] = new[:, :RANK]
            user[at + PACK : at + CHUNK, :] = new[:, RANK:]
    out_ref[...] = user[...].T

    wait_bytes(items.at[0], item_sems.at[0])
    for chunk in range(CHUNKS):
        swaps[chunk].wait_send()

    def wait_sent(step, chunk, half, blocks, sem):
        if blocks:
            at = pl.ds(0, blocks), pl.ds(0, rows_of(step, chunk))
            wait_bytes(plane.at[(step, chunk, half, *at)], sem.at[step, chunk, half])

    @on(0)
    def _():
        for chunk in range(CHUNKS):
            wait_bytes(held.at[0, chunk], held_send.at[chunk])
            for half in range(2):
                wait_bytes(half_src.at[chunk, half, pl.ds(0, rows_of(0, chunk))], half_send.at[chunk, half])
            for step in range(1, ITERS):
                wait_sent(step, chunk, 0, FULL, plane_send)

    @on(1)
    def _():
        for chunk in range(CHUNKS):
            for half in range(2):
                wait_bytes(final.at[half, chunk], final_send.at[chunk, half])
            for step in range(ITERS):
                for half in range(2):
                    wait_sent(step, chunk, half, FULL - 1 if half or not step else 0, plane_send)
                    wait_sent(step, chunk, half, len(ring_targets(step, half)), ring_send)


def per_device(counts, user_factor, item_factor, week_factor):
    most = PACK + 8
    dma = pltpu.SemaphoreType.DMA
    each = (ITERS, CHUNKS, 2)
    arrays = counts, user_factor.T, item_factor.T, week_factor
    turned = pl.pallas_call(
        kernel,
        out_shape=pltpu.VMEM((RANK, USERS), F32),
        in_specs=[pl.BlockSpec(memory_space=pltpu.HBM)] * 4,
        out_specs=pl.BlockSpec(memory_space=pltpu.VMEM),
        scratch_shapes=[
            pltpu.VMEM((USERS + HALF, WEEKS, ITEMS), jnp.int32),
            pltpu.VMEM((RANK, USERS), F32),
            pltpu.VMEM((USERS, RANK), F32),
            pltpu.VMEM((2, RANK, ITEMS), F32),
            pltpu.VMEM((WEEKS, RANK), F32),
            pltpu.VMEM((WEEKS, 2 * RANK), F32),
            pltpu.VMEM((2, 4 * RANK, ITEMS), BF16),
            pltpu.VMEM((2, ITEMS, 2 * RANK), BF16),
            pltpu.VMEM((2, BLOCK * WEEKS, ITEMS), F32),
            pltpu.VMEM((2, CHUNKS, CHUNK, 2 * RANK), F32),
            pltpu.VMEM((2, CHUNK, 2 * RANK), F32),
            pltpu.VMEM((2, CHUNKS, PACK, 2 * RANK), F32),
            pltpu.VMEM((2, CHUNKS, PACK, 2 * RANK), F32),
            pltpu.VMEM((CHUNKS, 2, most, 2 * RANK), F32),
            pltpu.VMEM((CHUNKS, 2, most, 2 * RANK), F32),
            pltpu.VMEM((*each, FULL, most, 2 * RANK), F32),
            pltpu.VMEM((*each, Z, most, 2 * RANK), F32),
            dma((3,)), dma((len(range(0, USERS, BLOCK)),)), dma((2,)), dma((CHUNKS,)), dma((CHUNKS,)),
            dma((CHUNKS,)), dma((CHUNKS,)), dma((CHUNKS, 2)), dma((CHUNKS, 2)), dma((CHUNKS, 2)), dma((CHUNKS, 2)),
            dma(each), dma(each), dma(each), dma(each),
        ],
        compiler_params=pltpu.CompilerParams(
            collective_id=0, has_side_effects=True, vmem_limit_bytes=48 << 20
        ),
        name="updates",
    )(*[pltpu.with_memory_space_constraint(a, pltpu.HBM) for a in arrays])
    return turned.T


def solution(mesh):
    placed = (P(None, "week", "item"), P(), P("item", None), P("week", None))
    return jax.shard_map(per_device, mesh=mesh, in_specs=placed, out_specs=P(), check_vma=False)
```

```python
import jax
import jax.numpy as jnp
from jax import lax
from jax.experimental import pallas as pl
from jax.experimental.pallas import tpu as pltpu
from jax.sharding import PartitionSpec as P

MESH = pl.DeviceIdType.MESH
F32, BF16 = jnp.float32, jnp.bfloat16
ITERS = 3
USERS, RANK, WEEKS, ITEMS = 128, 64, 64, 256
HALF, CHUNK, BLOCK = 64, 32, 16
CHUNKS, BLOCKS = HALF // CHUNK, CHUNK // BLOCK
PACK = CHUNK // 2
X, Y, Z = 4, 4, 8
FULL = X * Y


def by_distance(offsets, sizes):
    far = lambda o: sum(min(d, n - d) for d, n in zip(o, sizes))
    return sorted(offsets, key=far, reverse=True)


PLANE = by_distance([(dx, dy) for dx in range(X) for dy in range(Y)], (X, Y))
RING = by_distance([(dz,) for dz in range(Z)], (Z,))


def rows_of(step, chunk):
    return PACK + 8 if step == 0 and chunk == 0 else PACK


def kernel(
    counts_hbm, user_hbm, item_hbm, week_hbm, out_ref,
    raw_counts, counts, user_turned, user, items, week, pair_week, model_rhs, phi_rhs, models, factor, phi, held, final,
    half_src, half_dst, plane, ring,
    load_sem, count_sem, item_sems, swap_send, swap_recv, held_send, held_recv, final_send, final_recv,
    half_send, half_recv, plane_send, plane_recv, ring_send, ring_recv,
):
    item, z_hi = lax.axis_index("item"), lax.axis_index("week")
    core, flat = lax.rem(item, 2), lax.rem(item // 2, FULL)
    x, y = lax.rem(flat, X), flat // X
    z = z_hi * 2 + item // (2 * FULL)

    def on(c):
        return pl.when(core == c)

    def in_plane(c, dx, dy):
        there = lax.rem(y + dy, Y) * X + lax.rem(x + dx, X)
        return {"item": item - core + c + (there - flat) * 2, "week": z_hi}

    def in_ring(c, dz):
        there = lax.rem(z + dz, Z)
        return {"item": lax.rem(there, 2) * (2 * FULL) + flat * 2 + c, "week": there // 2}

    other = in_ring(1 - core, 0)
    plane_peers = [[in_plane(c, *o) for o in PLANE] for c in range(2)]
    ring_peers = [[in_ring(c, *o) for o in RING] for c in range(2)]

    def remote(src, dst, send, recv, peer):
        return pltpu.make_async_remote_copy(
            src_ref=src, dst_ref=dst, send_sem=send, recv_sem=recv, device_id=peer, device_id_type=MESH
        )

    loads = [
        pltpu.make_async_copy(src, dst, load_sem.at[i])
        for i, (src, dst) in enumerate(((item_hbm, items.at[0]), (week_hbm, week), (user_hbm, user_turned)))
    ]
    for load in loads:
        load.start()
    barrier = pltpu.get_barrier_semaphore()

    def greet(peers):
        for peer in peers:
            pl.semaphore_signal(barrier, inc=1, device_id=peer, device_id_type=MESH)

    @on(0)
    def _():
        greet(ring_peers[1])

    @on(1)
    def _():
        greet(plane_peers[1][:-1] + ring_peers[1][:-1] + [other])

    first_blocks = [
        (chunk, half, b * BLOCK) for chunk in range(CHUNKS) for half in range(2) for b in range(BLOCKS)
    ]
    count_loads = []
    for i, (chunk, half, row) in enumerate(first_blocks):
        at = pl.ds(half * HALF + chunk * CHUNK + row, BLOCK)
        load = pltpu.make_async_copy(counts_hbm.at[at], raw_counts.at[at], count_sem.at[i])
        load.start()
        count_loads.append(load)
    for load in loads:
        load.wait()

    left = lax.broadcasted_iota(jnp.int32, (1, 2 * RANK), 1) < RANK

    def build_rhs(which):
        values = items[which]
        high = values.astype(BF16).astype(F32)
        low = values - high
        model_rhs[which] = jnp.concatenate([high, low, high, low], axis=0).astype(BF16)
        both = jnp.concatenate([high, low], axis=0).T
        phi_rhs[which] = both.astype(BF16)
        sums = jnp.sum(both, axis=0, keepdims=True)
        return sums + pltpu.roll(sums, RANK, 1)

    item_sums = build_rhs(0)
    weeks = week[...]
    pair_week[...] = jnp.concatenate([weeks, weeks], axis=1)
    share = jnp.broadcast_to(item_sums * jnp.sum(pair_week[...], axis=0, keepdims=True), (8, 2 * RANK))
    user[...] = user_turned[...].T

    for half in range(2):
        for chunk in range(CHUNKS):
            rows = user[half * HALF + chunk * CHUNK : half * HALF + (chunk + 1) * CHUNK, :]
            factor[half, chunk] = jnp.concatenate([rows, rows], axis=1)
            held[half, chunk] = jnp.concatenate([rows[:PACK], rows[PACK:]], axis=1)

    def model(block):
        _, half, chunk, row, which, _, _ = block
        w = pair_week[...]
        highs, lows = [], []
        for u in range(BLOCK):
            scaled = factor[half, chunk, row + u : row + u + 1, :] * w
            high = scaled.astype(BF16)
            highs.append(high)
            lows.append((scaled - high.astype(F32)).astype(BF16))
        lhs = jnp.concatenate([jnp.concatenate(highs, axis=0), jnp.concatenate(lows, axis=0)], axis=1)
        return jnp.dot(lhs, model_rhs[which], preferred_element_type=F32)

    def accumulate(block, slot):
        start, _, _, row, which, into, later_on = block
        if later_on is None:
            c = raw_counts[pl.ds(start, BLOCK)].astype(F32)
            counts[pl.ds(start, BLOCK)] = c
        else:
            c = counts[pl.ds(start, BLOCK)]
        c = c.reshape(BLOCK * WEEKS, ITEMS)
        ratio = c * pl.reciprocal(models[slot], approx=False)
        high = ratio.astype(BF16)
        low = (ratio - high.astype(F32)).astype(BF16)
        rhs = phi_rhs[which]
        sums = jnp.dot(
            jnp.concatenate([high, low], axis=1),
            jnp.concatenate([rhs, rhs], axis=0),
            preferred_element_type=F32,
        )
        sums = jnp.sum(sums.reshape(BLOCK, WEEKS, 2 * RANK) * pair_week[...][None], axis=1)
        if later_on:
            sums = sums + phi[into, row : row + BLOCK, :]
        phi[into, row : row + BLOCK, :] = sums

    def pack(half):
        both = phi[half]
        both = both + pltpu.roll(both, RANK, 1)
        return jnp.where(left, both[:PACK], both[PACK:])

    def compute(blocks, before, after):
        for j, block in enumerate(blocks):
            before(j)
            if j == 0:
                models[0] = model(block)
            if j + 1 < len(blocks):
                coming = model(blocks[j + 1])
            accumulate(block, j % 2)
            if j + 1 < len(blocks):
                models[(j + 1) % 2] = coming
            after(j)

    def wait_bytes(ref, sem):
        pltpu.make_async_copy(ref, ref, sem).wait()

    def total(parts):
        while len(parts) > 1:
            parts = [a + b for a, b in zip(parts[::2], parts[1::2])]
        return parts[0]

    def share_half(chunk, half):
        n = rows_of(0, chunk)
        mine = pack(half)
        half_src[chunk, half, :PACK] = mine
        if n > PACK:
            half_src[chunk, half, PACK:n] = share

        @on(0)
        def _():
            at = pl.ds(0, n)
            remote(
                half_src.at[chunk, half, at], half_dst.at[chunk, half, at],
                half_send.at[chunk, half], half_recv.at[chunk, half], other,
            ).start()

    def send_first(chunk, half):
        n = rows_of(0, chunk)

        @on(1)
        def _():
            wait_bytes(half_dst.at[chunk, half, pl.ds(0, n)], half_recv.at[chunk, half])
            plane[0, chunk, half, flat, :n] = half_src[chunk, half, :n] + half_dst[chunk, half, :n]
            block = plane.at[0, chunk, half, flat, pl.ds(0, n)]
            for peer in plane_peers[1][:-1]:
                remote(block, block, plane_send.at[0, chunk, half], plane_recv.at[0, chunk, half], peer).start()

    def send_plane(step, chunk):
        plane[step, chunk, core, flat, :PACK] = pack(0)
        for c, peers in ((0, plane_peers[1]), (1, plane_peers[1][:-1])):

            @on(c)
            def _():
                block = plane.at[step, chunk, c, flat, pl.ds(0, PACK)]
                for peer in peers:
                    remote(block, block, plane_send.at[step, chunk, c], plane_recv.at[step, chunk, c], peer).start()

    def ring_targets(step, half):
        return ring_peers[0] if half == 0 and step < ITERS - 1 else ring_peers[1][:-1]

    def send_ring(step, chunk, half):
        n = rows_of(step, chunk)

        @on(1)
        def _():
            arriving = FULL if step and half == 0 else FULL - 1
            wait_bytes(plane.at[step, chunk, half, pl.ds(0, arriving), pl.ds(0, n)], plane_recv.at[step, chunk, half])
            ring[step, chunk, half, z, :n] = total([plane[step, chunk, half, j, :n] for j in range(FULL)])
            block = ring.at[step, chunk, half, z, pl.ds(0, n)]
            for peer in ring_targets(step, half):
                remote(block, block, ring_send.at[step, chunk, half], ring_recv.at[step, chunk, half], peer).start()

    def wait_ring(step, chunk, c, half):
        at = pl.ds(0, Z - c), pl.ds(0, rows_of(step, chunk))
        wait_bytes(ring.at[(step, chunk, half, *at)], ring_recv.at[step, chunk, half])

    def wait_sent(step, chunk, half, blocks, sem):
        at = pl.ds(0, blocks), pl.ds(0, rows_of(step, chunk))
        wait_bytes(plane.at[(step, chunk, half, *at)], sem.at[step, chunk, half])

    def done_sending(step, sem):
        if step and sem is plane_send:

            @on(0)
            def _():
                for chunk in range(CHUNKS):
                    wait_sent(step, chunk, 0, FULL, sem)

        @on(1)
        def _():
            for chunk in range(CHUNKS):
                for half in range(2):
                    if sem is ring_send:
                        wait_sent(step, chunk, half, len(ring_targets(step, half)), sem)
                    elif half or not step:
                        wait_sent(step, chunk, half, FULL - 1, sem)

    denominator = {}

    def update(step, chunk):
        n = rows_of(step, chunk)
        for c in range(2):

            @on(c)
            def _():
                wait_ring(step, chunk, c, c)

        sums = total([ring[step, chunk, core, j, :n] for j in range(Z)])
        if n > PACK:
            denominator[0] = sums[PACK : PACK + 1]
        new = held[core, chunk] * sums[:PACK] / denominator[0]
        held[core, chunk] = new
        turned = pltpu.roll(new, RANK, 1)
        factor[core, chunk, :PACK] = jnp.where(left, new, turned)
        factor[core, chunk, PACK:] = jnp.where(left, turned, new)
        if step == ITERS - 2:

            @on(0)
            def _():
                mine = held.at[0, chunk]
                remote(mine, mine, held_send.at[chunk], held_recv.at[chunk], other).start()


    def before_first(j):
        if j % BLOCKS == 0:
            for load in count_loads[j : j + BLOCKS]:
                load.wait()

    def after_first(j):
        chunk, half, row = first_blocks[j]
        if row + BLOCK < CHUNK:
            return
        if chunk == 0 and half == 0:
            for c, n in ((0, 1), (1, FULL - 1 + Z - 1 + Z)):

                @on(c)
                def _():
                    pl.semaphore_wait(barrier, n)

        share_half(chunk, half)
        if half:
            send_first(chunk, 0)
        elif chunk:
            send_first(chunk - 1, 1)

    blocks = [
        (half * HALF + chunk * CHUNK + row, half, chunk, row, 0, half, None) for chunk, half, row in first_blocks
    ]
    compute(blocks, before_first, after_first)
    remote(items.at[0], items.at[1], item_sems.at[0], item_sems.at[1], other).start()
    swaps = []
    for chunk in range(CHUNKS):
        theirs = pl.ds(pl.multiple_of((1 - core) * HALF + chunk * CHUNK, CHUNK), CHUNK)
        landing = pl.ds(USERS + chunk * CHUNK, CHUNK)
        swap = remote(counts.at[theirs], counts.at[landing], swap_send.at[chunk], swap_recv.at[chunk], other)
        swap.start()
        swaps.append(swap)
    wait_bytes(items.at[1], item_sems.at[1])
    build_rhs(1)
    send_first(CHUNKS - 1, 1)
    for chunk in range(CHUNKS):
        for half in range(2):
            send_ring(0, chunk, half)

    def later(chunk):
        own = pl.multiple_of(core * HALF + chunk * CHUNK, CHUNK)
        blocks = [
            (start + row, core, chunk, row, which, 0, which > 0)
            for which, start in enumerate((own, USERS + chunk * CHUNK))
            for row in range(0, CHUNK, BLOCK)
        ]
        compute(blocks, lambda j: None, lambda j: None)

    for step in range(1, ITERS):
        for chunk in range(CHUNKS):
            update(step - 1, chunk)
            if step == 1:
                swaps[chunk].wait_recv()
            later(chunk)
            send_plane(step, chunk)
        done_sending(step - 1, plane_send)
        done_sending(step - 1, ring_send)
        if step == 1:
            wait_bytes(items.at[0], item_sems.at[0])
            for swap in swaps:
                swap.wait_send()

            @on(0)
            def _():
                for chunk in range(CHUNKS):
                    for half in range(2):
                        wait_bytes(half_src.at[chunk, half, pl.ds(0, rows_of(0, chunk))], half_send.at[chunk, half])

        if step == ITERS - 1:

            @on(0)
            def _():
                for chunk in range(CHUNKS):
                    wait_bytes(held.at[0, chunk], held_send.at[chunk])

        for chunk in range(CHUNKS):
            send_ring(step, chunk, 1)
            send_ring(step, chunk, 0)
    done_sending(ITERS - 1, plane_send)

    @on(1)
    def _():
        for chunk in range(CHUNKS):
            wait_bytes(held.at[0, chunk], held_recv.at[chunk])
            for half in (1, 0):
                wait_ring(ITERS - 1, chunk, 1, half)
                sums = total([ring[ITERS - 1, chunk, half, j, :PACK] for j in range(Z)])
                final[half, chunk] = held[half, chunk] * sums / denominator[0]
                mine = final.at[half, chunk]
                remote(mine, mine, final_send.at[chunk, half], final_recv.at[chunk, half], other).start()

    @on(0)
    def _():
        for chunk in range(CHUNKS):
            for half in (1, 0):
                wait_bytes(final.at[half, chunk], final_recv.at[chunk, half])

    for chunk in range(CHUNKS):
        for half in range(2):
            new = final[half, chunk]
            at = half * HALF + chunk * CHUNK
            user[at : at + PACK, :] = new[:, :RANK]
            user[at + PACK : at + CHUNK, :] = new[:, RANK:]
    out_ref[...] = user[...].T

    done_sending(ITERS - 1, ring_send)

    @on(1)
    def _():
        for chunk in range(CHUNKS):
            for half in range(2):
                wait_bytes(final.at[half, chunk], final_send.at[chunk, half])


def per_device(counts, user_factor, item_factor, week_factor):
    most = PACK + 8
    dma = pltpu.SemaphoreType.DMA
    each = (ITERS, CHUNKS, 2)
    arrays = counts, user_factor.T, item_factor.T, week_factor
    turned = pl.pallas_call(
        kernel,
        out_shape=pltpu.VMEM((RANK, USERS), F32),
        in_specs=[pl.BlockSpec(memory_space=pltpu.HBM)] * 4,
        out_specs=pl.BlockSpec(memory_space=pltpu.VMEM),
        scratch_shapes=[
            pltpu.VMEM((USERS, WEEKS, ITEMS), jnp.int32),
            pltpu.VMEM((USERS + HALF, WEEKS, ITEMS), F32),
            pltpu.VMEM((RANK, USERS), F32),
            pltpu.VMEM((USERS, RANK), F32),
            pltpu.VMEM((2, RANK, ITEMS), F32),
            pltpu.VMEM((WEEKS, RANK), F32),
            pltpu.VMEM((WEEKS, 2 * RANK), F32),
            pltpu.VMEM((2, 4 * RANK, ITEMS), BF16),
            pltpu.VMEM((2, ITEMS, 2 * RANK), BF16),
            pltpu.VMEM((2, BLOCK * WEEKS, ITEMS), F32),
            pltpu.VMEM((2, CHUNKS, CHUNK, 2 * RANK), F32),
            pltpu.VMEM((2, CHUNK, 2 * RANK), F32),
            pltpu.VMEM((2, CHUNKS, PACK, 2 * RANK), F32),
            pltpu.VMEM((2, CHUNKS, PACK, 2 * RANK), F32),
            pltpu.VMEM((CHUNKS, 2, most, 2 * RANK), F32),
            pltpu.VMEM((CHUNKS, 2, most, 2 * RANK), F32),
            pltpu.VMEM((*each, FULL, most, 2 * RANK), F32),
            pltpu.VMEM((*each, Z, most, 2 * RANK), F32),
            dma((3,)), dma((len(range(0, USERS, BLOCK)),)), dma((2,)), dma((CHUNKS,)), dma((CHUNKS,)),
            dma((CHUNKS,)), dma((CHUNKS,)), dma((CHUNKS, 2)), dma((CHUNKS, 2)), dma((CHUNKS, 2)), dma((CHUNKS, 2)),
            dma(each), dma(each), dma(each), dma(each),
        ],
        compiler_params=pltpu.CompilerParams(
            collective_id=0, has_side_effects=True, vmem_limit_bytes=48 << 20
        ),
        name="updates",
    )(*[pltpu.with_memory_space_constraint(a, pltpu.HBM) for a in arrays])
    return turned.T


def solution(mesh):
    placed = (P(None, "week", "item"), P(), P("item", None), P("week", None))
    return jax.shard_map(per_device, mesh=mesh, in_specs=placed, out_specs=P(), check_vma=False)
```

```python
import jax
import jax.numpy as jnp
from jax import lax
from jax.experimental import pallas as pl
from jax.experimental.pallas import tpu as pltpu
from jax.sharding import PartitionSpec as P

MESH = pl.DeviceIdType.MESH
F32, BF16 = jnp.float32, jnp.bfloat16
ITERS = 3
USERS, RANK, WEEKS, ITEMS = 128, 64, 64, 256
HALF, CHUNK, BLOCK = 64, 32, 8
CHUNKS, BLOCKS = HALF // CHUNK, CHUNK // BLOCK
PACK = CHUNK // 2
X, Y, Z = 4, 4, 8
FULL = X * Y


def by_distance(offsets, sizes):
    far = lambda o: sum(min(d, n - d) for d, n in zip(o, sizes))
    return sorted(offsets, key=far, reverse=True)


PLANE = by_distance([(dx, dy) for dx in range(X) for dy in range(Y)], (X, Y))
RING = by_distance([(dz,) for dz in range(Z)], (Z,))


def rows_of(step, chunk):
    return PACK + 8 if step == 0 and chunk == 0 else PACK


def kernel(
    counts_hbm, user_hbm, item_hbm, week_hbm, out_ref,
    raw_counts, counts, user_turned, user, items, week, pair_week, model_rhs, phi_rhs, models, factor, phi, held, final,
    half_src, half_dst, plane, ring,
    load_sem, count_sem, item_sems, swap_send, swap_recv, held_send, held_recv, final_send, final_recv,
    half_send, half_recv, plane_send, plane_recv, ring_send, ring_recv,
):
    item, z_hi = lax.axis_index("item"), lax.axis_index("week")
    core, flat = lax.rem(item, 2), lax.rem(item // 2, FULL)
    x, y = lax.rem(flat, X), flat // X
    z = z_hi * 2 + item // (2 * FULL)

    def on(c):
        return pl.when(core == c)

    def in_plane(c, dx, dy):
        there = lax.rem(y + dy, Y) * X + lax.rem(x + dx, X)
        return {"item": item - core + c + (there - flat) * 2, "week": z_hi}

    def in_ring(c, dz):
        there = lax.rem(z + dz, Z)
        return {"item": lax.rem(there, 2) * (2 * FULL) + flat * 2 + c, "week": there // 2}

    other = in_ring(1 - core, 0)
    plane_peers = [[in_plane(c, *o) for o in PLANE] for c in range(2)]
    ring_peers = [[in_ring(c, *o) for o in RING] for c in range(2)]

    def remote(src, dst, send, recv, peer):
        return pltpu.make_async_remote_copy(
            src_ref=src, dst_ref=dst, send_sem=send, recv_sem=recv, device_id=peer, device_id_type=MESH
        )

    loads = [
        pltpu.make_async_copy(src, dst, load_sem.at[i])
        for i, (src, dst) in enumerate(((item_hbm, items.at[0]), (week_hbm, week), (user_hbm, user_turned)))
    ]
    for load in loads:
        load.start()
    barrier = pltpu.get_barrier_semaphore()

    def greet(peers):
        for peer in peers:
            pl.semaphore_signal(barrier, inc=1, device_id=peer, device_id_type=MESH)

    @on(0)
    def _():
        greet(ring_peers[1])

    @on(1)
    def _():
        greet(plane_peers[1][:-1] + ring_peers[1][:-1] + [other])

    first_blocks = [
        (chunk, half, b * BLOCK) for chunk in range(CHUNKS) for half in range(2) for b in range(BLOCKS)
    ]
    count_loads = []
    for i, (chunk, half, row) in enumerate(first_blocks):
        at = pl.ds(half * HALF + chunk * CHUNK + row, BLOCK)
        load = pltpu.make_async_copy(counts_hbm.at[at], raw_counts.at[at], count_sem.at[i])
        load.start()
        count_loads.append(load)
    for load in loads:
        load.wait()

    left = lax.broadcasted_iota(jnp.int32, (1, 2 * RANK), 1) < RANK

    def build_rhs(which):
        values = items[which]
        high = values.astype(BF16).astype(F32)
        low = values - high
        model_rhs[which] = jnp.concatenate([high, low, high, low], axis=0).astype(BF16)
        both = jnp.concatenate([high, low], axis=0).T
        phi_rhs[which] = both.astype(BF16)
        sums = jnp.sum(both, axis=0, keepdims=True)
        return sums + pltpu.roll(sums, RANK, 1)

    item_sums = build_rhs(0)
    weeks = week[...]
    pair_week[...] = jnp.concatenate([weeks, weeks], axis=1)
    share = jnp.broadcast_to(item_sums * jnp.sum(pair_week[...], axis=0, keepdims=True), (8, 2 * RANK))
    user[...] = user_turned[...].T

    for half in range(2):
        for chunk in range(CHUNKS):
            rows = user[half * HALF + chunk * CHUNK : half * HALF + (chunk + 1) * CHUNK, :]
            factor[half, chunk] = jnp.concatenate([rows, rows], axis=1)
            held[half, chunk] = jnp.concatenate([rows[:PACK], rows[PACK:]], axis=1)

    def model(block):
        _, half, chunk, row, which, _, _ = block
        w = pair_week[...]
        highs, lows = [], []
        for u in range(BLOCK):
            scaled = factor[half, chunk, row + u : row + u + 1, :] * w
            high = scaled.astype(BF16)
            highs.append(high)
            lows.append((scaled - high.astype(F32)).astype(BF16))
        lhs = jnp.concatenate([jnp.concatenate(highs, axis=0), jnp.concatenate(lows, axis=0)], axis=1)
        return jnp.dot(lhs, model_rhs[which], preferred_element_type=F32)

    def accumulate(block, slot):
        start, _, _, row, which, into, later_on = block
        if later_on is None:
            c = raw_counts[pl.ds(start, BLOCK)].astype(F32)
            counts[pl.ds(start, BLOCK)] = c
        else:
            c = counts[pl.ds(start, BLOCK)]
        c = c.reshape(BLOCK * WEEKS, ITEMS)
        ratio = c * pl.reciprocal(models[slot], approx=False)
        high = ratio.astype(BF16)
        low = (ratio - high.astype(F32)).astype(BF16)
        rhs = phi_rhs[which]
        sums = jnp.dot(
            jnp.concatenate([high, low], axis=1),
            jnp.concatenate([rhs, rhs], axis=0),
            preferred_element_type=F32,
        )
        sums = jnp.sum(sums.reshape(BLOCK, WEEKS, 2 * RANK) * pair_week[...][None], axis=1)
        if later_on:
            sums = sums + phi[into, row : row + BLOCK, :]
        phi[into, row : row + BLOCK, :] = sums

    def pack(half):
        both = phi[half]
        both = both + pltpu.roll(both, RANK, 1)
        return jnp.where(left, both[:PACK], both[PACK:])

    def compute(blocks, before, after):
        for j, block in enumerate(blocks):
            before(j)
            if j == 0:
                models[0] = model(block)
            if j + 1 < len(blocks):
                coming = model(blocks[j + 1])
            accumulate(block, j % 2)
            if j + 1 < len(blocks):
                models[(j + 1) % 2] = coming
            after(j)

    def wait_bytes(ref, sem):
        pltpu.make_async_copy(ref, ref, sem).wait()

    def total(parts):
        while len(parts) > 1:
            parts = [a + b for a, b in zip(parts[::2], parts[1::2])]
        return parts[0]

    def share_half(chunk, half):
        n = rows_of(0, chunk)
        mine = pack(half)
        half_src[chunk, half, :PACK] = mine
        if n > PACK:
            half_src[chunk, half, PACK:n] = share

        @on(0)
        def _():
            at = pl.ds(0, n)
            remote(
                half_src.at[chunk, half, at], half_dst.at[chunk, half, at],
                half_send.at[chunk, half], half_recv.at[chunk, half], other,
            ).start()

    def send_first(chunk, half):
        n = rows_of(0, chunk)

        @on(1)
        def _():
            wait_bytes(half_dst.at[chunk, half, pl.ds(0, n)], half_recv.at[chunk, half])
            plane[0, chunk, half, flat, :n] = half_src[chunk, half, :n] + half_dst[chunk, half, :n]
            block = plane.at[0, chunk, half, flat, pl.ds(0, n)]
            for peer in plane_peers[1][:-1]:
                remote(block, block, plane_send.at[0, chunk, half], plane_recv.at[0, chunk, half], peer).start()

    def send_plane(step, chunk):
        plane[step, chunk, core, flat, :PACK] = pack(0)
        for c, peers in ((0, plane_peers[1]), (1, plane_peers[1][:-1])):

            @on(c)
            def _():
                block = plane.at[step, chunk, c, flat, pl.ds(0, PACK)]
                for peer in peers:
                    remote(block, block, plane_send.at[step, chunk, c], plane_recv.at[step, chunk, c], peer).start()

    def ring_targets(step, half):
        return ring_peers[0] if half == 0 and step < ITERS - 1 else ring_peers[1][:-1]

    def send_ring(step, chunk, half):
        n = rows_of(step, chunk)

        @on(1)
        def _():
            arriving = FULL if step and half == 0 else FULL - 1
            wait_bytes(plane.at[step, chunk, half, pl.ds(0, arriving), pl.ds(0, n)], plane_recv.at[step, chunk, half])
            ring[step, chunk, half, z, :n] = total([plane[step, chunk, half, j, :n] for j in range(FULL)])
            block = ring.at[step, chunk, half, z, pl.ds(0, n)]
            for peer in ring_targets(step, half):
                remote(block, block, ring_send.at[step, chunk, half], ring_recv.at[step, chunk, half], peer).start()

    def wait_ring(step, chunk, c, half):
        at = pl.ds(0, Z - c), pl.ds(0, rows_of(step, chunk))
        wait_bytes(ring.at[(step, chunk, half, *at)], ring_recv.at[step, chunk, half])

    def wait_sent(step, chunk, half, blocks, sem):
        at = pl.ds(0, blocks), pl.ds(0, rows_of(step, chunk))
        wait_bytes(plane.at[(step, chunk, half, *at)], sem.at[step, chunk, half])

    def done_sending(step, sem):
        if step and sem is plane_send:

            @on(0)
            def _():
                for chunk in range(CHUNKS):
                    wait_sent(step, chunk, 0, FULL, sem)

        @on(1)
        def _():
            for chunk in range(CHUNKS):
                for half in range(2):
                    if sem is ring_send:
                        wait_sent(step, chunk, half, len(ring_targets(step, half)), sem)
                    elif half or not step:
                        wait_sent(step, chunk, half, FULL - 1, sem)

    denominator = {}

    def update(step, chunk):
        n = rows_of(step, chunk)
        for c in range(2):

            @on(c)
            def _():
                wait_ring(step, chunk, c, c)

        sums = total([ring[step, chunk, core, j, :n] for j in range(Z)])
        if n > PACK:
            denominator[0] = sums[PACK : PACK + 1]
        new = held[core, chunk] * sums[:PACK] / denominator[0]
        held[core, chunk] = new
        turned = pltpu.roll(new, RANK, 1)
        factor[core, chunk, :PACK] = jnp.where(left, new, turned)
        factor[core, chunk, PACK:] = jnp.where(left, turned, new)

    def before_first(j):
        if j % BLOCKS == 0:
            for load in count_loads[j : j + BLOCKS]:
                load.wait()

    def after_first(j):
        chunk, half, row = first_blocks[j]
        if row + BLOCK < CHUNK:
            return
        if chunk == 0:

            @on(half)
            def _():
                pl.semaphore_wait(barrier, (FULL - 1 + Z - 1 + Z) if half else 1)

        share_half(chunk, half)
        if half:
            send_first(chunk, 0)
        elif chunk:
            send_first(chunk - 1, 1)

    blocks = [
        (half * HALF + chunk * CHUNK + row, half, chunk, row, 0, half, None) for chunk, half, row in first_blocks
    ]
    compute(blocks, before_first, after_first)
    remote(items.at[0], items.at[1], item_sems.at[0], item_sems.at[1], other).start()
    swaps = []
    for chunk in range(CHUNKS):
        theirs = pl.ds(pl.multiple_of((1 - core) * HALF + chunk * CHUNK, CHUNK), CHUNK)
        landing = pl.ds(USERS + chunk * CHUNK, CHUNK)
        swap = remote(counts.at[theirs], counts.at[landing], swap_send.at[chunk], swap_recv.at[chunk], other)
        swap.start()
        swaps.append(swap)
    wait_bytes(items.at[1], item_sems.at[1])
    build_rhs(1)
    send_first(CHUNKS - 1, 1)
    for chunk in range(CHUNKS):
        for half in range(2):
            send_ring(0, chunk, half)

    def later(chunk):
        own = pl.multiple_of(core * HALF + chunk * CHUNK, CHUNK)
        blocks = [
            (start + row, core, chunk, row, which, 0, which > 0)
            for which, start in enumerate((own, USERS + chunk * CHUNK))
            for row in range(0, CHUNK, BLOCK)
        ]
        compute(blocks, lambda j: None, lambda j: None)

    for step in range(1, ITERS):
        for chunk in range(CHUNKS):
            if step == 1:
                swaps[chunk].wait_recv()
            update(step - 1, chunk)
            later(chunk)
            send_plane(step, chunk)
            if step == ITERS - 1:

                @on(0)
                def _():
                    mine = held.at[0, chunk]
                    remote(mine, mine, held_send.at[chunk], held_recv.at[chunk], other).start()

        done_sending(step - 1, plane_send)
        done_sending(step - 1, ring_send)
        if step == 1:
            wait_bytes(items.at[0], item_sems.at[0])
            for swap in swaps:
                swap.wait_send()

            @on(0)
            def _():
                for chunk in range(CHUNKS):
                    for half in range(2):
                        wait_bytes(half_src.at[chunk, half, pl.ds(0, rows_of(0, chunk))], half_send.at[chunk, half])

        if step == ITERS - 1:

            @on(0)
            def _():
                for chunk in range(CHUNKS):
                    wait_bytes(held.at[0, chunk], held_send.at[chunk])

        for chunk in range(CHUNKS):
            send_ring(step, chunk, 1)
            send_ring(step, chunk, 0)
    done_sending(ITERS - 1, plane_send)

    @on(1)
    def _():
        for chunk in range(CHUNKS):
            wait_bytes(held.at[0, chunk], held_recv.at[chunk])
            for half in (1, 0):
                wait_ring(ITERS - 1, chunk, 1, half)
                sums = total([ring[ITERS - 1, chunk, half, j, :PACK] for j in range(Z)])
                final[half, chunk] = held[half, chunk] * sums / denominator[0]
                mine = final.at[half, chunk]
                remote(mine, mine, final_send.at[chunk, half], final_recv.at[chunk, half], other).start()

    @on(0)
    def _():
        for chunk in range(CHUNKS):
            for half in (1, 0):
                wait_bytes(final.at[half, chunk], final_recv.at[chunk, half])

    for chunk in range(CHUNKS):
        for half in range(2):
            new = final[half, chunk]
            at = half * HALF + chunk * CHUNK
            user[at : at + PACK, :] = new[:, :RANK]
            user[at + PACK : at + CHUNK, :] = new[:, RANK:]
    out_ref[...] = user[...].T

    done_sending(ITERS - 1, ring_send)

    @on(1)
    def _():
        for chunk in range(CHUNKS):
            for half in range(2):
                wait_bytes(final.at[half, chunk], final_send.at[chunk, half])


def per_device(counts, user_factor, item_factor, week_factor):
    most = PACK + 8
    dma = pltpu.SemaphoreType.DMA
    each = (ITERS, CHUNKS, 2)
    arrays = counts, user_factor.T, item_factor.T, week_factor
    turned = pl.pallas_call(
        kernel,
        out_shape=pltpu.VMEM((RANK, USERS), F32),
        in_specs=[pl.BlockSpec(memory_space=pltpu.HBM)] * 4,
        out_specs=pl.BlockSpec(memory_space=pltpu.VMEM),
        scratch_shapes=[
            pltpu.VMEM((USERS, WEEKS, ITEMS), jnp.int32),
            pltpu.VMEM((USERS + HALF, WEEKS, ITEMS), F32),
            pltpu.VMEM((RANK, USERS), F32),
            pltpu.VMEM((USERS, RANK), F32),
            pltpu.VMEM((2, RANK, ITEMS), F32),
            pltpu.VMEM((WEEKS, RANK), F32),
            pltpu.VMEM((WEEKS, 2 * RANK), F32),
            pltpu.VMEM((2, 4 * RANK, ITEMS), BF16),
            pltpu.VMEM((2, ITEMS, 2 * RANK), BF16),
            pltpu.VMEM((2, BLOCK * WEEKS, ITEMS), F32),
            pltpu.VMEM((2, CHUNKS, CHUNK, 2 * RANK), F32),
            pltpu.VMEM((2, CHUNK, 2 * RANK), F32),
            pltpu.VMEM((2, CHUNKS, PACK, 2 * RANK), F32),
            pltpu.VMEM((2, CHUNKS, PACK, 2 * RANK), F32),
            pltpu.VMEM((CHUNKS, 2, most, 2 * RANK), F32),
            pltpu.VMEM((CHUNKS, 2, most, 2 * RANK), F32),
            pltpu.VMEM((*each, FULL, most, 2 * RANK), F32),
            pltpu.VMEM((*each, Z, most, 2 * RANK), F32),
            dma((3,)), dma((len(range(0, USERS, BLOCK)),)), dma((2,)), dma((CHUNKS,)), dma((CHUNKS,)),
            dma((CHUNKS,)), dma((CHUNKS,)), dma((CHUNKS, 2)), dma((CHUNKS, 2)), dma((CHUNKS, 2)), dma((CHUNKS, 2)),
            dma(each), dma(each), dma(each), dma(each),
        ],
        compiler_params=pltpu.CompilerParams(
            collective_id=0, has_side_effects=True, vmem_limit_bytes=48 << 20
        ),
        name="updates",
    )(*[pltpu.with_memory_space_constraint(a, pltpu.HBM) for a in arrays])
    return turned.T


def solution(mesh):
    placed = (P(None, "week", "item"), P(), P("item", None), P("week", None))
    return jax.shard_map(per_device, mesh=mesh, in_specs=placed, out_specs=P(), check_vma=False)
```

```python
import jax
import jax.numpy as jnp
from jax import lax
from jax.experimental import pallas as pl
from jax.experimental.pallas import tpu as pltpu
from jax.sharding import PartitionSpec as P

MESH = pl.DeviceIdType.MESH
F32, BF16 = jnp.float32, jnp.bfloat16
ITERS = 3
USERS, RANK, WEEKS, ITEMS = 128, 64, 64, 256
HALF, CHUNK, BLOCK = 64, 32, 8
CHUNKS, BLOCKS = HALF // CHUNK, CHUNK // BLOCK
PACK = CHUNK // 2
X, Y, Z = 4, 4, 8
FULL = X * Y


def by_distance(offsets, sizes):
    far = lambda o: sum(min(d, n - d) for d, n in zip(o, sizes))
    return sorted(offsets, key=far, reverse=True)


PLANE = by_distance([(dx, dy) for dx in range(X) for dy in range(Y)], (X, Y))
RING = by_distance([(dz,) for dz in range(Z)], (Z,))


def rows_of(step, chunk):
    return PACK + 8 if step == 0 and chunk == 0 else PACK


def kernel(
    counts_hbm, user_hbm, item_hbm, week_hbm, out_ref,
    raw_counts, counts, user_turned, user, items, week, pair_week, model_rhs, phi_rhs, models, factor, phi, held, final,
    half_src, half_dst, plane, ring,
    load_sem, count_sem, item_sems, swap_send, swap_recv, held_send, held_recv, final_send, final_recv,
    half_send, half_recv, plane_send, plane_recv, ring_send, ring_recv,
):
    item, z_hi = lax.axis_index("item"), lax.axis_index("week")
    core, flat = lax.rem(item, 2), lax.rem(item // 2, FULL)
    x, y = lax.rem(flat, X), flat // X
    z = z_hi * 2 + item // (2 * FULL)

    def on(c):
        return pl.when(core == c)

    def in_plane(c, dx, dy):
        there = lax.rem(y + dy, Y) * X + lax.rem(x + dx, X)
        return {"item": item - core + c + (there - flat) * 2, "week": z_hi}

    def in_ring(c, dz):
        there = lax.rem(z + dz, Z)
        return {"item": lax.rem(there, 2) * (2 * FULL) + flat * 2 + c, "week": there // 2}

    other = in_ring(1 - core, 0)
    plane_peers = [[in_plane(c, *o) for o in PLANE] for c in range(2)]
    ring_peers = [[in_ring(c, *o) for o in RING] for c in range(2)]

    def remote(src, dst, send, recv, peer):
        return pltpu.make_async_remote_copy(
            src_ref=src, dst_ref=dst, send_sem=send, recv_sem=recv, device_id=peer, device_id_type=MESH
        )

    loads = [
        pltpu.make_async_copy(src, dst, load_sem.at[i])
        for i, (src, dst) in enumerate(((item_hbm, items.at[0]), (week_hbm, week), (user_hbm, user_turned)))
    ]
    for load in loads:
        load.start()
    barrier = pltpu.get_barrier_semaphore()

    def greet(peers):
        for peer in peers:
            pl.semaphore_signal(barrier, inc=1, device_id=peer, device_id_type=MESH)

    @on(0)
    def _():
        greet(ring_peers[1])

    @on(1)
    def _():
        greet(plane_peers[1][:-1] + ring_peers[1][:-1] + [other])

    first_blocks = [
        (chunk, half, b * BLOCK) for chunk in range(CHUNKS) for half in range(2) for b in range(BLOCKS)
    ]
    count_loads = []
    for i, (chunk, half, row) in enumerate(first_blocks):
        at = pl.ds(half * HALF + chunk * CHUNK + row, BLOCK)
        load = pltpu.make_async_copy(counts_hbm.at[at], raw_counts.at[at], count_sem.at[i])
        load.start()
        count_loads.append(load)
    for load in loads:
        load.wait()

    left = lax.broadcasted_iota(jnp.int32, (1, 2 * RANK), 1) < RANK

    def build_rhs(which):
        values = items[which]
        high = values.astype(BF16).astype(F32)
        low = values - high
        model_rhs[which] = jnp.concatenate([high, low, high, low], axis=0).astype(BF16)
        both = jnp.concatenate([high, low], axis=0).T
        phi_rhs[which] = both.astype(BF16)
        sums = jnp.sum(both, axis=0, keepdims=True)
        return sums + pltpu.roll(sums, RANK, 1)

    item_sums = build_rhs(0)
    weeks = week[...]
    pair_week[...] = jnp.concatenate([weeks, weeks], axis=1)
    share = jnp.broadcast_to(item_sums * jnp.sum(pair_week[...], axis=0, keepdims=True), (8, 2 * RANK))
    user[...] = user_turned[...].T

    for half in range(2):
        for chunk in range(CHUNKS):
            rows = user[half * HALF + chunk * CHUNK : half * HALF + (chunk + 1) * CHUNK, :]
            factor[half, chunk] = jnp.concatenate([rows, rows], axis=1)
            held[half, chunk] = jnp.concatenate([rows[:PACK], rows[PACK:]], axis=1)

    def model(block):
        _, half, chunk, row, which, _, _ = block
        w = pair_week[...]
        highs, lows = [], []
        for u in range(BLOCK):
            scaled = factor[half, chunk, row + u : row + u + 1, :] * w
            high = scaled.astype(BF16)
            highs.append(high)
            lows.append((scaled - high.astype(F32)).astype(BF16))
        lhs = jnp.concatenate([jnp.concatenate(highs, axis=0), jnp.concatenate(lows, axis=0)], axis=1)
        return jnp.dot(lhs, model_rhs[which], preferred_element_type=F32)

    def accumulate(block, slot):
        start, _, _, row, which, into, later_on = block
        if later_on is None:
            c = raw_counts[pl.ds(start, BLOCK)].astype(F32)
            counts[pl.ds(start, BLOCK)] = c
        else:
            c = counts[pl.ds(start, BLOCK)]
        c = c.reshape(BLOCK * WEEKS, ITEMS)
        ratio = c * pl.reciprocal(models[slot], approx=False)
        high = ratio.astype(BF16)
        low = (ratio - high.astype(F32)).astype(BF16)
        rhs = phi_rhs[which]
        sums = jnp.dot(
            jnp.concatenate([high, low], axis=1),
            jnp.concatenate([rhs, rhs], axis=0),
            preferred_element_type=F32,
        )
        sums = jnp.sum(sums.reshape(BLOCK, WEEKS, 2 * RANK) * pair_week[...][None], axis=1)
        if later_on:
            sums = sums + phi[into, row : row + BLOCK, :]
        phi[into, row : row + BLOCK, :] = sums

    def pack(half):
        both = phi[half]
        both = both + pltpu.roll(both, RANK, 1)
        return jnp.where(left, both[:PACK], both[PACK:])

    def compute(blocks, before, after):
        for j, block in enumerate(blocks):
            before(j)
            if j == 0:
                models[0] = model(block)
            if j + 1 < len(blocks):
                coming = model(blocks[j + 1])
            accumulate(block, j % 2)
            if j + 1 < len(blocks):
                models[(j + 1) % 2] = coming
            after(j)

    def wait_bytes(ref, sem):
        pltpu.make_async_copy(ref, ref, sem).wait()

    def total(parts):
        while len(parts) > 1:
            parts = [a + b for a, b in zip(parts[::2], parts[1::2])]
        return parts[0]

    def share_half(chunk, half):
        n = rows_of(0, chunk)
        mine = pack(half)
        half_src[chunk, half, :PACK] = mine
        if n > PACK:
            half_src[chunk, half, PACK:n] = share

        @on(0)
        def _():
            at = pl.ds(0, n)
            remote(
                half_src.at[chunk, half, at], half_dst.at[chunk, half, at],
                half_send.at[chunk, half], half_recv.at[chunk, half], other,
            ).start()

    def send_first(chunk, half):
        n = rows_of(0, chunk)

        @on(1)
        def _():
            wait_bytes(half_dst.at[chunk, half, pl.ds(0, n)], half_recv.at[chunk, half])
            plane[0, chunk, half, flat, :n] = half_src[chunk, half, :n] + half_dst[chunk, half, :n]
            block = plane.at[0, chunk, half, flat, pl.ds(0, n)]
            for peer in plane_peers[1][:-1]:
                remote(block, block, plane_send.at[0, chunk, half], plane_recv.at[0, chunk, half], peer).start()

    def send_plane(step, chunk):
        plane[step, chunk, core, flat, :PACK] = pack(0)
        for c, peers in ((0, plane_peers[1]), (1, plane_peers[1][:-1])):

            @on(c)
            def _():
                block = plane.at[step, chunk, c, flat, pl.ds(0, PACK)]
                for peer in peers:
                    remote(block, block, plane_send.at[step, chunk, c], plane_recv.at[step, chunk, c], peer).start()

    def to_both(step, chunk, half):
        return (step, chunk, half) == (ITERS - 1, CHUNKS - 1, 0)

    def ring_targets(step, chunk, half):
        if to_both(step, chunk, half):
            return ring_peers[1][:-1] + ring_peers[0]
        return ring_peers[0] if half == 0 and step < ITERS - 1 else ring_peers[1][:-1]

    def send_ring(step, chunk, half):
        n = rows_of(step, chunk)

        @on(1)
        def _():
            arriving = FULL if step and half == 0 else FULL - 1
            wait_bytes(plane.at[step, chunk, half, pl.ds(0, arriving), pl.ds(0, n)], plane_recv.at[step, chunk, half])
            ring[step, chunk, half, z, :n] = total([plane[step, chunk, half, j, :n] for j in range(FULL)])
            block = ring.at[step, chunk, half, z, pl.ds(0, n)]
            for peer in ring_targets(step, chunk, half):
                remote(block, block, ring_send.at[step, chunk, half], ring_recv.at[step, chunk, half], peer).start()

    def wait_ring(step, chunk, c, half):
        at = pl.ds(0, Z - c), pl.ds(0, rows_of(step, chunk))
        wait_bytes(ring.at[(step, chunk, half, *at)], ring_recv.at[step, chunk, half])

    def wait_sent(step, chunk, half, blocks, sem):
        at = pl.ds(0, blocks), pl.ds(0, rows_of(step, chunk))
        wait_bytes(plane.at[(step, chunk, half, *at)], sem.at[step, chunk, half])

    def done_sending(step, sem):
        if step and sem is plane_send:

            @on(0)
            def _():
                for chunk in range(CHUNKS):
                    wait_sent(step, chunk, 0, FULL, sem)

        @on(1)
        def _():
            for chunk in range(CHUNKS):
                for half in range(2):
                    if sem is ring_send:
                        wait_sent(step, chunk, half, len(ring_targets(step, chunk, half)), sem)
                    elif half or not step:
                        wait_sent(step, chunk, half, FULL - 1, sem)

    denominator = {}

    def update(step, chunk):
        n = rows_of(step, chunk)
        for c in range(2):

            @on(c)
            def _():
                wait_ring(step, chunk, c, c)

        sums = total([ring[step, chunk, core, j, :n] for j in range(Z)])
        if n > PACK:
            denominator[0] = sums[PACK : PACK + 1]
        new = held[core, chunk] * sums[:PACK] / denominator[0]
        held[core, chunk] = new
        turned = pltpu.roll(new, RANK, 1)
        factor[core, chunk, :PACK] = jnp.where(left, new, turned)
        factor[core, chunk, PACK:] = jnp.where(left, turned, new)

    def before_first(j):
        if j % BLOCKS == 0:
            for load in count_loads[j : j + BLOCKS]:
                load.wait()

    def after_first(j):
        chunk, half, row = first_blocks[j]
        if row + BLOCK < CHUNK:
            return
        if chunk == 0:

            @on(half)
            def _():
                pl.semaphore_wait(barrier, (FULL - 1 + Z - 1 + Z) if half else 1)

        share_half(chunk, half)
        if half:
            send_first(chunk, 0)
        elif chunk:
            send_first(chunk - 1, 1)

    blocks = [
        (half * HALF + chunk * CHUNK + row, half, chunk, row, 0, half, None) for chunk, half, row in first_blocks
    ]
    compute(blocks, before_first, after_first)
    remote(items.at[0], items.at[1], item_sems.at[0], item_sems.at[1], other).start()
    swaps = []
    for chunk in range(CHUNKS):
        theirs = pl.ds(pl.multiple_of((1 - core) * HALF + chunk * CHUNK, CHUNK), CHUNK)
        landing = pl.ds(USERS + chunk * CHUNK, CHUNK)
        swap = remote(counts.at[theirs], counts.at[landing], swap_send.at[chunk], swap_recv.at[chunk], other)
        swap.start()
        swaps.append(swap)
    wait_bytes(items.at[1], item_sems.at[1])
    build_rhs(1)
    send_first(CHUNKS - 1, 1)
    for chunk in range(CHUNKS):
        for half in range(2):
            send_ring(0, chunk, half)

    def later(chunk):
        own = pl.multiple_of(core * HALF + chunk * CHUNK, CHUNK)
        blocks = [
            (start + row, core, chunk, row, which, 0, which > 0)
            for which, start in enumerate((own, USERS + chunk * CHUNK))
            for row in range(0, CHUNK, BLOCK)
        ]
        compute(blocks, lambda j: None, lambda j: None)

    for step in range(1, ITERS):
        for chunk in range(CHUNKS):
            if step == 1:
                swaps[chunk].wait_recv()
            update(step - 1, chunk)
            later(chunk)
            send_plane(step, chunk)
            if step == ITERS - 1:

                @on(0)
                def _():
                    mine = held.at[0, chunk]
                    remote(mine, mine, held_send.at[chunk], held_recv.at[chunk], other).start()

        done_sending(step - 1, plane_send)
        done_sending(step - 1, ring_send)
        if step == 1:
            wait_bytes(items.at[0], item_sems.at[0])
            for swap in swaps:
                swap.wait_send()

            @on(0)
            def _():
                for chunk in range(CHUNKS):
                    for half in range(2):
                        wait_bytes(half_src.at[chunk, half, pl.ds(0, rows_of(0, chunk))], half_send.at[chunk, half])

        if step == ITERS - 1:

            @on(0)
            def _():
                for chunk in range(CHUNKS):
                    wait_bytes(held.at[0, chunk], held_send.at[chunk])

        for chunk in range(CHUNKS):
            send_ring(step, chunk, 1)
            send_ring(step, chunk, 0)
    done_sending(ITERS - 1, plane_send)

    def finish(c, chunk, half):
        wait_ring(ITERS - 1, chunk, c, half)
        sums = total([ring[ITERS - 1, chunk, half, j, :PACK] for j in range(Z)])
        final[half, chunk] = held[half, chunk] * sums / denominator[0]

    pieces = [(chunk, half) for chunk in range(CHUNKS) for half in (1, 0)]

    @on(1)
    def _():
        for chunk, half in pieces:
            if half == 0:
                wait_bytes(held.at[0, chunk], held_recv.at[chunk])
            finish(1, chunk, half)
            if not to_both(ITERS - 1, chunk, half):
                mine = final.at[half, chunk]
                remote(mine, mine, final_send.at[chunk, half], final_recv.at[chunk, half], other).start()

    @on(0)
    def _():
        for chunk, half in pieces:
            if to_both(ITERS - 1, chunk, half):
                finish(0, chunk, half)
            else:
                wait_bytes(final.at[half, chunk], final_recv.at[chunk, half])

    for chunk in range(CHUNKS):
        for half in range(2):
            new = final[half, chunk]
            at = half * HALF + chunk * CHUNK
            user[at : at + PACK, :] = new[:, :RANK]
            user[at + PACK : at + CHUNK, :] = new[:, RANK:]
    out_ref[...] = user[...].T

    done_sending(ITERS - 1, ring_send)

    @on(1)
    def _():
        for chunk, half in pieces:
            if not to_both(ITERS - 1, chunk, half):
                wait_bytes(final.at[half, chunk], final_send.at[chunk, half])


def per_device(counts, user_factor, item_factor, week_factor):
    most = PACK + 8
    dma = pltpu.SemaphoreType.DMA
    each = (ITERS, CHUNKS, 2)
    arrays = counts, user_factor.T, item_factor.T, week_factor
    turned = pl.pallas_call(
        kernel,
        out_shape=pltpu.VMEM((RANK, USERS), F32),
        in_specs=[pl.BlockSpec(memory_space=pltpu.HBM)] * 4,
        out_specs=pl.BlockSpec(memory_space=pltpu.VMEM),
        scratch_shapes=[
            pltpu.VMEM((USERS, WEEKS, ITEMS), jnp.int32),
            pltpu.VMEM((USERS + HALF, WEEKS, ITEMS), F32),
            pltpu.VMEM((RANK, USERS), F32),
            pltpu.VMEM((USERS, RANK), F32),
            pltpu.VMEM((2, RANK, ITEMS), F32),
            pltpu.VMEM((WEEKS, RANK), F32),
            pltpu.VMEM((WEEKS, 2 * RANK), F32),
            pltpu.VMEM((2, 4 * RANK, ITEMS), BF16),
            pltpu.VMEM((2, ITEMS, 2 * RANK), BF16),
            pltpu.VMEM((2, BLOCK * WEEKS, ITEMS), F32),
            pltpu.VMEM((2, CHUNKS, CHUNK, 2 * RANK), F32),
            pltpu.VMEM((2, CHUNK, 2 * RANK), F32),
            pltpu.VMEM((2, CHUNKS, PACK, 2 * RANK), F32),
            pltpu.VMEM((2, CHUNKS, PACK, 2 * RANK), F32),
            pltpu.VMEM((CHUNKS, 2, most, 2 * RANK), F32),
            pltpu.VMEM((CHUNKS, 2, most, 2 * RANK), F32),
            pltpu.VMEM((*each, FULL, most, 2 * RANK), F32),
            pltpu.VMEM((*each, Z, most, 2 * RANK), F32),
            dma((3,)), dma((len(range(0, USERS, BLOCK)),)), dma((2,)), dma((CHUNKS,)), dma((CHUNKS,)),
            dma((CHUNKS,)), dma((CHUNKS,)), dma((CHUNKS, 2)), dma((CHUNKS, 2)), dma((CHUNKS, 2)), dma((CHUNKS, 2)),
            dma(each), dma(each), dma(each), dma(each),
        ],
        compiler_params=pltpu.CompilerParams(
            collective_id=0, has_side_effects=True, vmem_limit_bytes=48 << 20
        ),
        name="updates",
    )(*[pltpu.with_memory_space_constraint(a, pltpu.HBM) for a in arrays])
    return turned.T


def solution(mesh):
    placed = (P(None, "week", "item"), P(), P("item", None), P("week", None))
    return jax.shard_map(per_device, mesh=mesh, in_specs=placed, out_specs=P(), check_vma=False)
```

```python
import jax
import jax.numpy as jnp
from jax import lax
from jax.experimental import pallas as pl
from jax.experimental.pallas import tpu as pltpu
from jax.sharding import PartitionSpec as P

MESH = pl.DeviceIdType.MESH
F32, BF16 = jnp.float32, jnp.bfloat16
ITERS = 3
USERS, RANK, WEEKS, ITEMS = 128, 64, 64, 256
HALF, CHUNK, BLOCK = 64, 32, 8
CHUNKS, BLOCKS = HALF // CHUNK, CHUNK // BLOCK
PACK = CHUNK // 2
X, Y, Z = 4, 4, 8
FULL = X * Y


def by_distance(offsets, sizes):
    far = lambda o: sum(min(d, n - d) for d, n in zip(o, sizes))
    return sorted(offsets, key=far, reverse=True)


PLANE = by_distance([(dx, dy) for dx in range(X) for dy in range(Y)], (X, Y))
RING = by_distance([(dz,) for dz in range(Z)], (Z,))


def rows_of(step, chunk):
    return PACK + 8 if step == 0 and chunk == 0 else PACK


def kernel(
    counts_hbm, user_hbm, item_hbm, week_hbm, out_ref,
    raw_counts, counts, user_turned, user, items, week, pair_week, model_rhs, phi_rhs, models, factor, phi, held, final,
    half_src, half_dst, plane, ring,
    load_sem, count_sem, item_sems, swap_send, swap_recv, held_send, held_recv, final_send, final_recv,
    half_send, half_recv, plane_send, plane_recv, ring_send, ring_recv,
):
    item, z_hi = lax.axis_index("item"), lax.axis_index("week")
    core, flat = lax.rem(item, 2), lax.rem(item // 2, FULL)
    x, y = lax.rem(flat, X), flat // X
    z = z_hi * 2 + item // (2 * FULL)

    def on(c):
        return pl.when(core == c)

    def in_plane(c, dx, dy):
        there = lax.rem(y + dy, Y) * X + lax.rem(x + dx, X)
        return {"item": item - core + c + (there - flat) * 2, "week": z_hi}

    def in_ring(c, dz):
        there = lax.rem(z + dz, Z)
        return {"item": lax.rem(there, 2) * (2 * FULL) + flat * 2 + c, "week": there // 2}

    other = in_ring(1 - core, 0)
    plane_peers = [[in_plane(c, *o) for o in PLANE] for c in range(2)]
    ring_peers = [[in_ring(c, *o) for o in RING] for c in range(2)]

    def remote(src, dst, send, recv, peer):
        return pltpu.make_async_remote_copy(
            src_ref=src, dst_ref=dst, send_sem=send, recv_sem=recv, device_id=peer, device_id_type=MESH
        )

    loads = [
        pltpu.make_async_copy(src, dst, load_sem.at[i])
        for i, (src, dst) in enumerate(((item_hbm, items.at[0]), (week_hbm, week), (user_hbm, user_turned)))
    ]
    for load in loads:
        load.start()
    barrier = pltpu.get_barrier_semaphore()

    def greet(peers):
        for peer in peers:
            pl.semaphore_signal(barrier, inc=1, device_id=peer, device_id_type=MESH)

    @on(0)
    def _():
        greet(ring_peers[1])

    @on(1)
    def _():
        greet(plane_peers[1][:-1] + ring_peers[1][:-1] + [other])

    first_blocks = [
        (chunk, half, b * BLOCK) for chunk in range(CHUNKS) for half in range(2) for b in range(BLOCKS)
    ]
    count_loads = []
    for i, (chunk, half, row) in enumerate(first_blocks):
        at = pl.ds(half * HALF + chunk * CHUNK + row, BLOCK)
        load = pltpu.make_async_copy(counts_hbm.at[at], raw_counts.at[at], count_sem.at[i])
        load.start()
        count_loads.append(load)
    for load in loads:
        load.wait()

    left = lax.broadcasted_iota(jnp.int32, (1, 2 * RANK), 1) < RANK

    def build_rhs(which):
        values = items[which]
        high = values.astype(BF16).astype(F32)
        low = values - high
        model_rhs[which] = jnp.concatenate([high, low, high, low], axis=0).astype(BF16)
        both = jnp.concatenate([high, low], axis=0).T
        phi_rhs[which] = both.astype(BF16)
        sums = jnp.sum(both, axis=0, keepdims=True)
        return sums + pltpu.roll(sums, RANK, 1)

    item_sums = build_rhs(0)
    weeks = week[...]
    pair_week[...] = jnp.concatenate([weeks, weeks], axis=1)
    share = jnp.broadcast_to(item_sums * jnp.sum(pair_week[...], axis=0, keepdims=True), (8, 2 * RANK))
    user[...] = user_turned[...].T

    for half in range(2):
        for chunk in range(CHUNKS):
            rows = user[half * HALF + chunk * CHUNK : half * HALF + (chunk + 1) * CHUNK, :]
            factor[half, chunk] = jnp.concatenate([rows, rows], axis=1)
            held[half, chunk] = jnp.concatenate([rows[:PACK], rows[PACK:]], axis=1)

    def model(block):
        _, half, chunk, row, which, _, _ = block
        w = pair_week[...]
        highs, lows = [], []
        for u in range(BLOCK):
            scaled = factor[half, chunk, row + u : row + u + 1, :] * w
            high = scaled.astype(BF16)
            highs.append(high)
            lows.append((scaled - high.astype(F32)).astype(BF16))
        lhs = jnp.concatenate([jnp.concatenate(highs, axis=0), jnp.concatenate(lows, axis=0)], axis=1)
        return jnp.dot(lhs, model_rhs[which], preferred_element_type=F32)

    def accumulate(block, slot):
        start, _, _, row, which, into, later_on = block
        if later_on is None:
            c = raw_counts[pl.ds(start, BLOCK)].astype(F32)
            counts[pl.ds(start, BLOCK)] = c
        else:
            c = counts[pl.ds(start, BLOCK)]
        c = c.reshape(BLOCK * WEEKS, ITEMS)
        ratio = c * pl.reciprocal(models[slot], approx=False)
        high = ratio.astype(BF16)
        low = (ratio - high.astype(F32)).astype(BF16)
        rhs = phi_rhs[which]
        sums = jnp.dot(
            jnp.concatenate([high, low], axis=1),
            jnp.concatenate([rhs, rhs], axis=0),
            preferred_element_type=F32,
        )
        sums = jnp.sum(sums.reshape(BLOCK, WEEKS, 2 * RANK) * pair_week[...][None], axis=1)
        if later_on:
            sums = sums + phi[into, row : row + BLOCK, :]
        phi[into, row : row + BLOCK, :] = sums

    def pack(half):
        both = phi[half]
        both = both + pltpu.roll(both, RANK, 1)
        return jnp.where(left, both[:PACK], both[PACK:])

    def compute(blocks, before, after):
        for j, block in enumerate(blocks):
            before(j)
            if j == 0:
                models[0] = model(block)
            if j + 1 < len(blocks):
                coming = model(blocks[j + 1])
            accumulate(block, j % 2)
            if j + 1 < len(blocks):
                models[(j + 1) % 2] = coming
            after(j)

    def wait_bytes(ref, sem):
        pltpu.make_async_copy(ref, ref, sem).wait()

    def total(parts):
        while len(parts) > 1:
            parts = [a + b for a, b in zip(parts[::2], parts[1::2])]
        return parts[0]

    def share_half(chunk, half):
        n = rows_of(0, chunk)
        mine = pack(half)
        half_src[chunk, half, :PACK] = mine
        if n > PACK:
            half_src[chunk, half, PACK:n] = share

        @on(0)
        def _():
            at = pl.ds(0, n)
            remote(
                half_src.at[chunk, half, at], half_dst.at[chunk, half, at],
                half_send.at[chunk, half], half_recv.at[chunk, half], other,
            ).start()

    def send_first(chunk, half):
        n = rows_of(0, chunk)

        @on(1)
        def _():
            wait_bytes(half_dst.at[chunk, half, pl.ds(0, n)], half_recv.at[chunk, half])
            plane[0, chunk, half, flat, :n] = half_src[chunk, half, :n] + half_dst[chunk, half, :n]
            block = plane.at[0, chunk, half, flat, pl.ds(0, n)]
            for peer in plane_peers[1][:-1]:
                remote(block, block, plane_send.at[0, chunk, half], plane_recv.at[0, chunk, half], peer).start()

    def send_plane(step, chunk):
        plane[step, chunk, core, flat, :PACK] = pack(0)
        for c, peers in ((0, plane_peers[1]), (1, plane_peers[1][:-1])):

            @on(c)
            def _():
                block = plane.at[step, chunk, c, flat, pl.ds(0, PACK)]
                for peer in peers:
                    remote(block, block, plane_send.at[step, chunk, c], plane_recv.at[step, chunk, c], peer).start()

    def to_both(step, chunk, half):
        return (step, chunk, half) == (ITERS - 1, CHUNKS - 1, 0)

    def ring_targets(step, chunk, half):
        if to_both(step, chunk, half):
            return ring_peers[1][:-1] + ring_peers[0]
        return ring_peers[0] if half == 0 and step < ITERS - 1 else ring_peers[1][:-1]

    def send_ring(step, chunk, half):
        n = rows_of(step, chunk)

        @on(1)
        def _():
            arriving = FULL if step and half == 0 else FULL - 1
            wait_bytes(plane.at[step, chunk, half, pl.ds(0, arriving), pl.ds(0, n)], plane_recv.at[step, chunk, half])
            ring[step, chunk, half, z, :n] = total([plane[step, chunk, half, j, :n] for j in range(FULL)])
            block = ring.at[step, chunk, half, z, pl.ds(0, n)]
            for peer in ring_targets(step, chunk, half):
                remote(block, block, ring_send.at[step, chunk, half], ring_recv.at[step, chunk, half], peer).start()

    def wait_ring(step, chunk, c, half):
        at = pl.ds(0, Z - c), pl.ds(0, rows_of(step, chunk))
        wait_bytes(ring.at[(step, chunk, half, *at)], ring_recv.at[step, chunk, half])

    def wait_sent(step, chunk, half, blocks, sem):
        at = pl.ds(0, blocks), pl.ds(0, rows_of(step, chunk))
        wait_bytes(plane.at[(step, chunk, half, *at)], sem.at[step, chunk, half])

    def done_sending(step, sem):
        if step and sem is plane_send:

            @on(0)
            def _():
                for chunk in range(CHUNKS):
                    wait_sent(step, chunk, 0, FULL, sem)

        @on(1)
        def _():
            for chunk in range(CHUNKS):
                for half in range(2):
                    if sem is ring_send:
                        wait_sent(step, chunk, half, len(ring_targets(step, chunk, half)), sem)
                    elif half or not step:
                        wait_sent(step, chunk, half, FULL - 1, sem)

    denominator = {}

    def update(step, chunk):
        n = rows_of(step, chunk)
        for c in range(2):

            @on(c)
            def _():
                wait_ring(step, chunk, c, c)

        sums = total([ring[step, chunk, core, j, :n] for j in range(Z)])
        if n > PACK:
            denominator[0] = sums[PACK : PACK + 1]
        new = held[core, chunk] * sums[:PACK] / denominator[0]
        held[core, chunk] = new
        turned = pltpu.roll(new, RANK, 1)
        factor[core, chunk, :PACK] = jnp.where(left, new, turned)
        factor[core, chunk, PACK:] = jnp.where(left, turned, new)

    def before_first(j):
        begin = 0 if j == 0 else BLOCKS // 2 if j == BLOCKS // 2 else j if j % BLOCKS == 0 else None
        if begin is not None:
            end = BLOCKS // 2 if j == 0 else BLOCKS if j == BLOCKS // 2 else j + BLOCKS
            for load in count_loads[begin:end]:
                load.wait()

    def after_first(j):
        chunk, half, row = first_blocks[j]
        if row + BLOCK < CHUNK:
            return
        if chunk == 0:

            @on(half)
            def _():
                pl.semaphore_wait(barrier, (FULL - 1 + Z - 1 + Z) if half else 1)

        share_half(chunk, half)
        if half:
            send_first(chunk, 0)
        elif chunk:
            send_first(chunk - 1, 1)

    blocks = [
        (half * HALF + chunk * CHUNK + row, half, chunk, row, 0, half, None) for chunk, half, row in first_blocks
    ]
    compute(blocks, before_first, after_first)
    remote(items.at[0], items.at[1], item_sems.at[0], item_sems.at[1], other).start()
    swaps = []
    for chunk in range(CHUNKS):
        theirs = pl.ds(pl.multiple_of((1 - core) * HALF + chunk * CHUNK, CHUNK), CHUNK)
        landing = pl.ds(USERS + chunk * CHUNK, CHUNK)
        swap = remote(counts.at[theirs], counts.at[landing], swap_send.at[chunk], swap_recv.at[chunk], other)
        swap.start()
        swaps.append(swap)
    wait_bytes(items.at[1], item_sems.at[1])
    build_rhs(1)
    send_first(CHUNKS - 1, 1)
    for chunk in range(CHUNKS):
        for half in range(2):
            send_ring(0, chunk, half)

    def later(chunk):
        own = pl.multiple_of(core * HALF + chunk * CHUNK, CHUNK)
        blocks = [
            (start + row, core, chunk, row, which, 0, which > 0)
            for which, start in enumerate((own, USERS + chunk * CHUNK))
            for row in range(0, CHUNK, BLOCK)
        ]
        compute(blocks, lambda j: None, lambda j: None)

    for step in range(1, ITERS):
        for chunk in range(CHUNKS):
            if step == 1:
                swaps[chunk].wait_recv()
            update(step - 1, chunk)
            later(chunk)
            send_plane(step, chunk)
            if step == ITERS - 1:

                @on(0)
                def _():
                    mine = held.at[0, chunk]
                    remote(mine, mine, held_send.at[chunk], held_recv.at[chunk], other).start()

        done_sending(step - 1, plane_send)
        done_sending(step - 1, ring_send)
        if step == 1:
            wait_bytes(items.at[0], item_sems.at[0])
            for swap in swaps:
                swap.wait_send()

            @on(0)
            def _():
                for chunk in range(CHUNKS):
                    for half in range(2):
                        wait_bytes(half_src.at[chunk, half, pl.ds(0, rows_of(0, chunk))], half_send.at[chunk, half])

        if step == ITERS - 1:

            @on(0)
            def _():
                for chunk in range(CHUNKS):
                    wait_bytes(held.at[0, chunk], held_send.at[chunk])

        for chunk in range(CHUNKS):
            send_ring(step, chunk, 1)
            send_ring(step, chunk, 0)
    done_sending(ITERS - 1, plane_send)

    def finish(c, chunk, half):
        wait_ring(ITERS - 1, chunk, c, half)
        sums = total([ring[ITERS - 1, chunk, half, j, :PACK] for j in range(Z)])
        final[half, chunk] = held[half, chunk] * sums / denominator[0]

    def place(chunk, half):
        new = final[half, chunk]
        at = half * HALF + chunk * CHUNK
        user[at : at + PACK, :] = new[:, :RANK]
        user[at + PACK : at + CHUNK, :] = new[:, RANK:]

    pieces = [(chunk, half) for chunk in range(CHUNKS) for half in (1, 0)]

    @on(1)
    def _():
        for chunk, half in pieces:
            if half == 0:
                wait_bytes(held.at[0, chunk], held_recv.at[chunk])
            finish(1, chunk, half)
            if not to_both(ITERS - 1, chunk, half):
                mine = final.at[half, chunk]
                remote(mine, mine, final_send.at[chunk, half], final_recv.at[chunk, half], other).start()
                place(chunk, half)

    @on(0)
    def _():
        for chunk, half in pieces:
            if to_both(ITERS - 1, chunk, half):
                finish(0, chunk, half)
            else:
                wait_bytes(final.at[half, chunk], final_recv.at[chunk, half])
                place(chunk, half)

    place(*pieces[-1])
    out_ref[...] = user[...].T

    done_sending(ITERS - 1, ring_send)

    @on(1)
    def _():
        for chunk, half in pieces:
            if not to_both(ITERS - 1, chunk, half):
                wait_bytes(final.at[half, chunk], final_send.at[chunk, half])


def per_device(counts, user_factor, item_factor, week_factor):
    most = PACK + 8
    dma = pltpu.SemaphoreType.DMA
    each = (ITERS, CHUNKS, 2)
    arrays = counts, user_factor.T, item_factor.T, week_factor
    turned = pl.pallas_call(
        kernel,
        out_shape=pltpu.VMEM((RANK, USERS), F32),
        in_specs=[pl.BlockSpec(memory_space=pltpu.HBM)] * 4,
        out_specs=pl.BlockSpec(memory_space=pltpu.VMEM),
        scratch_shapes=[
            pltpu.VMEM((USERS, WEEKS, ITEMS), jnp.int32),
            pltpu.VMEM((USERS + HALF, WEEKS, ITEMS), F32),
            pltpu.VMEM((RANK, USERS), F32),
            pltpu.VMEM((USERS, RANK), F32),
            pltpu.VMEM((2, RANK, ITEMS), F32),
            pltpu.VMEM((WEEKS, RANK), F32),
            pltpu.VMEM((WEEKS, 2 * RANK), F32),
            pltpu.VMEM((2, 4 * RANK, ITEMS), BF16),
            pltpu.VMEM((2, ITEMS, 2 * RANK), BF16),
            pltpu.VMEM((2, BLOCK * WEEKS, ITEMS), F32),
            pltpu.VMEM((2, CHUNKS, CHUNK, 2 * RANK), F32),
            pltpu.VMEM((2, CHUNK, 2 * RANK), F32),
            pltpu.VMEM((2, CHUNKS, PACK, 2 * RANK), F32),
            pltpu.VMEM((2, CHUNKS, PACK, 2 * RANK), F32),
            pltpu.VMEM((CHUNKS, 2, most, 2 * RANK), F32),
            pltpu.VMEM((CHUNKS, 2, most, 2 * RANK), F32),
            pltpu.VMEM((*each, FULL, most, 2 * RANK), F32),
            pltpu.VMEM((*each, Z, most, 2 * RANK), F32),
            dma((3,)), dma((len(range(0, USERS, BLOCK)),)), dma((2,)), dma((CHUNKS,)), dma((CHUNKS,)),
            dma((CHUNKS,)), dma((CHUNKS,)), dma((CHUNKS, 2)), dma((CHUNKS, 2)), dma((CHUNKS, 2)), dma((CHUNKS, 2)),
            dma(each), dma(each), dma(each), dma(each),
        ],
        compiler_params=pltpu.CompilerParams(
            collective_id=0, has_side_effects=True, vmem_limit_bytes=48 << 20
        ),
        name="updates",
    )(*[pltpu.with_memory_space_constraint(a, pltpu.HBM) for a in arrays])
    return turned.T


def solution(mesh):
    placed = (P(None, "week", "item"), P(), P("item", None), P("week", None))
    return jax.shard_map(per_device, mesh=mesh, in_specs=placed, out_specs=P(), check_vma=False)
```
